32 devices in a mesh: row: 8 (over y, x, core), col: 4 (over z).
Axes of the slice: x: 2, y: 2, z: 4, core: 2. Of those that a mesh axis runs over, the one named last changes fastest.
Arguments:
- features: bfloat16 [4096, 2048], P(('row', 'col')), may hold values from -20 to 20
- weight_one: bfloat16 [2048, 2048], replicated, may hold values from -0.25 to 0.25
- bias_one: float32 [2048], replicated, may hold values from -3 to 3
- weight_two: bfloat16 [2048, 2048], replicated, may hold values from -0.25 to 0.25
- bias_two: float32 [2048], replicated, may hold values from -3 to 3
- cotangent: bfloat16 [4096, 2048], P(('row', 'col')), may hold values from -6 to 6
- neighbours: int32 [4096, 16], P('row'), may hold values from -1 to 4095, as said below
- valid_mask: int32 [4096], P(('row', 'col')), may hold values from 0 to 1
Outputs:
- act: bfloat16 [4096, 2048], P(('row', 'col'))
- grad_input: bfloat16 [4096, 2048], P(('row', 'col'))
- grad_weight_one: float32 [2048, 2048], P(('row', 'col'))
- grad_bias_one: float32 [2048], P(('row', 'col'))
- grad_weight_two: float32 [2048, 2048], P(('row', 'col'))
- grad_bias_two: float32 [2048], P(('row', 'col'))
- rms_stats: float32 [2, 3], replicated
The draws below stay inside these ranges and needn't reach their ends.
Inputs may be any that keep to these rules, and one draw needn't show every extreme that they name: `neighbours`: an entry is a node that row i aggregates, or -1 for an empty slot. No entry names a node whose valid_mask is 0, and the rows of such nodes hold only -1.
All inputs are finite; a program needn't handle non-finite values.
Results may differ from the reference program's by a relative error of at most 0.012.
The reference program's roundings to bfloat16 on the way count: a program that leaves them out, or rounds other values in their place, can miss the bound.
Values may be sent and summed in bfloat16 or wider, within the bound.
No kernel may reach another device: no remote copies, remote signals or barrier semaphores. Data moves between devices by JAX's collectives and lax.ppermute only.
A program may use at most 192 MiB of HBM per device.

```python
import math
import jax
import jax.numpy as jnp
from jax import lax

F = 2048
NODE_DEV = 128
K = 16
NODES = 4096


def graph_draw(key):
    base = jax.random.fold_in(key, 11)
    keys = jax.random.split(base, 6)
    nodes = jnp.arange(NODES, dtype=jnp.int32)
    validity = jax.random.randint(keys[0], (NODES,), 0, 10) > 0
    hole = jax.random.randint(keys[1], (), 1, NODES - 1)
    validity = validity & (nodes != hole) | (nodes == 0) | (nodes == NODES - 1)
    degree = jax.random.randint(keys[2], (NODES, 1), 0, K + 1)
    slots = jnp.arange(K, dtype=jnp.int32)[None, :]
    far = jax.random.randint(keys[3], (NODES, K), 0, 4) == 0
    shift = jax.random.randint(keys[4], (NODES, K), -NODE_DEV, NODE_DEV + 1)
    near = jnp.clip(nodes[:, None] + shift, 0, NODES - 1)
    anywhere = jax.random.randint(keys[5], (NODES, K), 0, NODES)
    chosen = jnp.where(far, anywhere, near)
    keep = (slots < degree) & validity[:, None] & validity[chosen]
    lists = jnp.where(keep, chosen, -1)
    lists = lists.at[0, 0].set(NODES - 1)
    return (lists.astype(jnp.int32), validity.astype(jnp.int32))


def draw_neighbours(key, part):
    return graph_draw(key)[0]


def draw_valid_mask(key, part):
    return graph_draw(key)[1]


def draw_features(key, part):
    keys = jax.random.split(jax.random.fold_in(key, 3), 2)
    place = jnp.arange(NODES, dtype=jnp.float32)[:, None] / NODES
    spread = jax.random.uniform(keys[0], (NODES, 1), jnp.float32, -0.5, 0.5)
    scale = 0.5 * jnp.exp(place * math.log(3.0) + spread * math.log(10.0))
    values = jnp.clip(jax.random.normal(keys[1], (NODES, F), jnp.float32), -4.0, 4.0)
    return (values * scale).astype(jnp.bfloat16)


def levels(rng, extent, shards, smallest, largest):
    def one(axis_at, parts):
        steps = jax.random.uniform(jax.random.fold_in(jax.random.fold_in(rng, 6), axis_at), (parts,), jnp.float32, smallest / len(shards), largest / len(shards))
        return jnp.repeat(jnp.exp(steps), extent[axis_at] // parts).reshape((-1,) + (1,) * (len(extent) - axis_at - 1))

    factor_of = one(*shards[0])
    for cut in shards[1:]:
        factor_of = factor_of * one(*cut)
    return factor_of


def scatter_about(rng, shape, scale, limit, cuts=(), kind=jnp.bfloat16):
    entries = jax.random.normal(rng, shape, jnp.float32) * scale
    if len(cuts) > 0:
        entries = levels(rng, shape, cuts, -0.22, 0.18) * entries
    return jnp.clip(entries, min=-limit, max=limit).astype(kind)


def setup_inputs(seed: int = 0) -> dict:
    splits = jax.random.split(jax.random.key(seed), 9)
    return {
        "features": draw_features(jax.random.fold_in(splits[8], 71), 0),
        "weight_one": scatter_about(splits[1], (F, F), (F // 4) ** -0.5, 0.25),
        "bias_one": scatter_about(splits[2], (F,), 0.5, 3.0, (), jnp.float32),
        "weight_two": scatter_about(splits[3], (F, F), (F // 4) ** -0.5, 0.25),
        "bias_two": scatter_about(splits[4], (F,), 0.5, 3.0, (), jnp.float32),
        "cotangent": scatter_about(splits[5], (NODES, F), 1.0, 6.0, ((0, 32),)),
        "neighbours": draw_neighbours(jax.random.fold_in(splits[8], 71), 0),
        "valid_mask": draw_valid_mask(jax.random.fold_in(splits[8], 71), 0),
    }


@jax.custom_vjp
def low(v):
    return lax.optimization_barrier(v.astype(jnp.bfloat16)).astype(jnp.float32)

@jax.custom_vjp
def low_back(v):
    return v

def low_keep(v):
    return (low(v), None)

def low_pass(kept, grad):
    return (grad,)

def back_keep(v):
    return (v, None)

def back_low(kept, grad):
    return (low(grad),)
low.defvjp(low_keep, low_pass)
low_back.defvjp(back_keep, back_low)

def neighbour_sums(inputs, lists):
    total = jnp.zeros_like(inputs)
    for slot in range(lists.shape[1]):
        index = lists[:, slot]
        picked = inputs[jnp.maximum(index, 0)]
        total = total + jnp.where((index >= 0)[:, None], picked, jnp.zeros_like(picked))
    return total

def one_layer(inputs, weight, bias, lists, inverse, validity):
    summed = low_back(neighbour_sums(inputs, lists))
    aggregate = low(low_back((summed + 2.0 * inputs) * inverse[:, None]))
    preact = jnp.dot(aggregate, weight, precision=lax.Precision.HIGHEST, preferred_element_type=jnp.float32)
    preact = low_back(preact + bias)
    output = validity[:, None] * jax.nn.gelu(preact, approximate=True)
    return (output, aggregate)

def reference(features, weight_one, bias_one, weight_two, bias_two, cotangent, neighbours, valid_mask):
    degree = lax.optimization_barrier(jnp.sum(neighbours >= 0, axis=1)).astype(jnp.float32)
    inverse = 1.0 / (degree + 1.0)
    validity = valid_mask.astype(jnp.float32)
    start = features.astype(jnp.float32)

    def forward(first, w_one, b_one, w_two, b_two):
        out_one, agg_one = one_layer(first, w_one, b_one, neighbours, inverse, validity)
        hidden = low(out_one)
        out_two, agg_two = one_layer(hidden, w_two, b_two, neighbours, inverse, validity)
        return (out_two, (agg_one, out_one, hidden, agg_two))
    out_two, pull, kept = jax.vjp(forward, start, weight_one.astype(jnp.float32), bias_one, weight_two.astype(jnp.float32), bias_two, has_aux=True)
    agg_one, out_one, hidden, agg_two = kept
    grad_start, grad_w_one, grad_b_one, grad_w_two, grad_b_two = pull(cotangent.astype(jnp.float32))

    def squares(value):
        return jnp.sum(validity[:, None] * value * value)
    totals = jnp.stack([squares(start), squares(agg_one), squares(out_one), squares(hidden), squares(agg_two), squares(out_two)]).reshape(2, 3)
    count = jnp.sum(validity) * start.shape[1]
    rms_stats = jnp.sqrt(totals / count + 1e-06)
    return (out_two.astype(jnp.bfloat16), grad_start.astype(jnp.bfloat16), grad_w_one, grad_b_one, grad_w_two, grad_b_two, rms_stats)
```

```python
import functools

import jax
import jax.numpy as jnp
from jax import lax
from jax.experimental import pallas as pl
from jax.experimental.pallas import tpu as pltpu
from jax.sharding import Mesh
from jax.sharding import PartitionSpec as P

BF16, F32 = jnp.bfloat16, jnp.float32
LANES = 128
MXU = 256
MIB = 1 << 20
NT = (((1,), (1,)), ((), ()))
GELU_C, GELU_A = 0.7978845608, 0.044715


def gelu_value(value):
    return jax.nn.gelu(value, approximate=True)


def source_parts(lists, per_dev, col_devs):
    live = lists >= 0
    safe = jnp.maximum(lists, 0)
    block = safe // per_dev
    return (live, block // col_devs, block % col_devs, safe % per_dev)


def count_tile(lists, usable, local_index, span):
    columns = jnp.arange(span, dtype=jnp.int32)[None, :]
    marked = jnp.where(usable, local_index, -1)
    total = jnp.zeros((lists.shape[0], span), jnp.float32)
    for slot in range(lists.shape[1]):
        total = total + (marked[:, slot : slot + 1] == columns).astype(jnp.float32)
    return total.astype(jnp.bfloat16)


def reduce_weights(grad_weight, grad_bias):
    return (
        lax.psum_scatter(grad_weight, ("row", "col"), scatter_dimension=0, tiled=True),
        lax.psum_scatter(grad_bias, ("row", "col"), scatter_dimension=0, tiled=True),
    )


def general(features, weight_one, bias_one, weight_two, bias_two, cotangent, neighbours, valid_mask):
    per_dev, width = features.shape
    row_devs = lax.axis_size("row")
    col_devs = lax.axis_size("col")
    col_pos = lax.axis_index("col")
    own_lists = lax.dynamic_slice_in_dim(neighbours, col_pos * per_dev, per_dev, 0)
    inverse = 1.0 / (jnp.sum(own_lists >= 0, axis=1).astype(jnp.float32) + 1.0)
    scaling = inverse[:, None]
    validity = valid_mask.astype(jnp.float32)[:, None]
    live, src_row, src_col, offset = source_parts(neighbours, per_dev, col_devs)
    front_tile = count_tile(
        neighbours, live & (src_col == col_pos), src_row * per_dev + offset, row_devs * per_dev
    )

    def forward_layer(inputs, weight, bias):
        gathered = lax.all_gather(inputs, "row", axis=0, tiled=True)
        partial_value = jnp.dot(front_tile, gathered, preferred_element_type=jnp.float32)
        summed = lax.psum_scatter(partial_value, "col", scatter_dimension=0, tiled=True)
        aggregate = ((summed + 2.0 * inputs.astype(jnp.float32)) * scaling).astype(jnp.bfloat16)
        preact = jnp.dot(aggregate, weight, preferred_element_type=jnp.float32) + bias
        return (aggregate, preact, validity * gelu_value(preact))

    agg_one, pre_one, out_one = forward_layer(features, weight_one, bias_one)
    hidden = out_one.astype(jnp.bfloat16)
    agg_two, pre_two, out_two = forward_layer(hidden, weight_two, bias_two)

    def squares(value):
        return jnp.sum(validity * jnp.square(value.astype(jnp.float32)))

    local_squares = jnp.stack(
        [
            squares(features),
            squares(agg_one),
            squares(out_one),
            squares(hidden),
            squares(agg_two),
            squares(out_two),
        ]
    ).reshape(2, 3)
    total_squares, total_valid = lax.psum((local_squares, jnp.sum(validity)), ("row", "col"))
    rms_stats = jnp.sqrt(total_squares / (total_valid * width) + 1e-06)

    def backward_layer(upstream, aggregate, preact, weight):
        grad_act = validity * upstream
        grad_pre = jax.vjp(gelu_value, preact)[1](grad_act)[0].astype(jnp.bfloat16)
        grad_weight = lax.dot_general(
            aggregate, grad_pre, (((0,), (0,)), ((), ())), preferred_element_type=jnp.float32
        )
        grad_bias = jnp.sum(grad_pre.astype(jnp.float32), axis=0)
        grad_low = lax.dot_general(
            grad_pre, weight, (((1,), (1,)), ((), ())), preferred_element_type=jnp.float32
        ).astype(jnp.bfloat16)
        grad_agg = lax.optimization_barrier(grad_low).astype(jnp.float32)
        grad_sum = (grad_agg * scaling).astype(jnp.bfloat16)
        grad_all = lax.all_gather(grad_sum, "col", axis=0, tiled=True)
        from_lists = lax.psum_scatter(
            lax.dot_general(
                front_tile, grad_all, (((0,), (0,)), ((), ())), preferred_element_type=jnp.float32
            ),
            "row",
            scatter_dimension=0,
            tiled=True,
        )
        return (from_lists + 2.0 * grad_agg * scaling, grad_weight, grad_bias)

    grad_hidden, weight_grad_two, bias_grad_two = backward_layer(
        cotangent.astype(jnp.float32), agg_two, pre_two, weight_two
    )
    weight_grad_two, bias_grad_two = reduce_weights(weight_grad_two, bias_grad_two)
    grad_start, weight_grad_one, bias_grad_one = backward_layer(
        grad_hidden, agg_one, pre_one, weight_one
    )
    weight_grad_one, bias_grad_one = reduce_weights(weight_grad_one, bias_grad_one)
    return (
        out_two.astype(jnp.bfloat16),
        grad_start.astype(jnp.bfloat16),
        weight_grad_one,
        bias_grad_one,
        weight_grad_two,
        bias_grad_two,
        rms_stats,
    )


def halves(value):
    high = value.astype(BF16)
    return high, (value - high.astype(F32)).astype(BF16)


def tile_kernel(high_ref, low_ref, tile_ref, inverse_ref):
    groups, lanes = high_ref.shape
    sources = tile_ref.shape[1]
    rows = tile_ref.shape[0] // groups
    place = lax.broadcasted_iota(jnp.int32, (MXU, lanes), 0)
    for group in range(groups):
        high = (place == high_ref[group : group + 1, :]).astype(F32).astype(BF16)
        low = (place == low_ref[group : group + 1, :]).astype(F32).astype(BF16)
        counts = lax.dot_general(high, low, NT, preferred_element_type=F32)
        at = slice(group * rows, (group + 1) * rows)
        total = jnp.zeros((rows, MXU), F32)
        for block in range(sources // MXU):
            piece = counts[block * rows : (block + 1) * rows]
            tile_ref[at, block * MXU : (block + 1) * MXU] = piece.astype(BF16)
            total = total + piece
        degree = jnp.sum(total, axis=1, keepdims=True)
        inverse_ref[at, :] = jnp.broadcast_to(1.0 / (degree + 1.0), (rows, LANES))


def count_tiles(high, low, sources):
    groups, lanes = high.shape
    rows = MXU * MXU // sources
    step = 8
    return pl.pallas_call(
        tile_kernel,
        grid=(groups // step,),
        in_specs=[pl.BlockSpec((step, lanes), lambda g: (g, 0))] * 2,
        out_specs=[
            pl.BlockSpec((step * rows, sources), lambda g: (g, 0)),
            pl.BlockSpec((step * rows, LANES), lambda g: (g, 0)),
        ],
        out_shape=[
            jax.ShapeDtypeStruct((groups * rows, sources), BF16),
            jax.ShapeDtypeStruct((groups * rows, LANES), F32),
        ],
        cost_estimate=pl.CostEstimate(
            flops=2 * groups * MXU * MXU * lanes,
            bytes_accessed=2 * groups * rows * sources,
            transcendentals=0,
        ),
    )(high, low)


def forward_kernel(tile_ref, own_ref, other_ref, rows_ref, inverse_ref, out_ref):
    half = own_ref.shape[0]
    total = jnp.dot(tile_ref[:, :half], own_ref[...], preferred_element_type=F32)
    total += jnp.dot(tile_ref[:, half:], other_ref[...], preferred_element_type=F32)
    total += 2.0 * rows_ref[...].astype(F32)
    out_ref[...] = (total * inverse_ref[...]).astype(BF16)


def apply_forward(tile, own, other, inverse):
    half, sources = tile.shape
    width = own.shape[1]
    step = half // 4
    return pl.pallas_call(
        forward_kernel,
        grid=(half // step,),
        in_specs=[
            pl.BlockSpec((step, sources), lambda i: (i, 0)),
            pl.BlockSpec((half, width), lambda i: (0, 0)),
            pl.BlockSpec((half, width), lambda i: (0, 0)),
            pl.BlockSpec((step, width), lambda i: (i, 0)),
            pl.BlockSpec((step, width), lambda i: (i, 0)),
        ],
        out_specs=pl.BlockSpec((step, width), lambda i: (i, 0)),
        out_shape=jax.ShapeDtypeStruct((half, width), BF16),
        cost_estimate=pl.CostEstimate(
            flops=4 * half * sources * width, bytes_accessed=2 * half * sources, transcendentals=0
        ),
    )(tile, own, other, own, inverse)


def backward_kernel(with_more, grad_ref, tile_ref, *refs):
    out_ref = refs[-1]
    grads = jnp.concatenate([grad_ref[i] for i in range(grad_ref.shape[0])], axis=1)
    total = jnp.dot(grads, tile_ref[...], preferred_element_type=F32)
    for at in range(out_ref.shape[0]):
        piece = total[:, at * LANES : (at + 1) * LANES]
        if with_more:
            piece = piece + refs[0][at].astype(F32)
        out_ref[at] = piece.astype(BF16)


def apply_backward(tile, grads, part, more=None):
    half, sources = tile.shape
    chips, width, nodes = grads.shape
    steps = 4
    block = chips // steps
    specs = [
        pl.BlockSpec((chips, width, nodes), lambda i: (0, 0, 0)),
        pl.BlockSpec((half, half // steps), lambda i: (0, part * steps + i)),
    ]
    operands = [grads, tile]
    if more is not None:
        specs.append(pl.BlockSpec((block, width, nodes), lambda i: (i, 0, 0)))
        operands.append(more)
    return pl.pallas_call(
        functools.partial(backward_kernel, more is not None),
        grid=(steps,),
        in_specs=specs,
        out_specs=pl.BlockSpec((block, width, nodes), lambda i: (i, 0, 0)),
        out_shape=jax.ShapeDtypeStruct((chips, width, nodes), BF16),
        cost_estimate=pl.CostEstimate(
            flops=4 * half * half * width, bytes_accessed=2 * half * half, transcendentals=0
        ),
    )(*operands)


def dense_kernel(last, agg_ref, weight_ref, bias_ref, valid_ref, input_ref, out_ref, slope_ref, stat_ref):
    step = pl.program_id(0)
    valid = valid_ref[...]
    agg = jnp.concatenate([agg_ref[i] for i in range(agg_ref.shape[0])], axis=1)
    pre = jnp.dot(agg, weight_ref[...], preferred_element_type=F32) + bias_ref[...]
    square = pre * pre
    bend = jnp.tanh(GELU_C * (pre + GELU_A * (square * pre)))
    out = valid * (0.5 * pre * (1.0 + bend))
    inner = GELU_C * (1.0 + 3.0 * GELU_A * square)
    slope_ref[...] = valid * (0.5 * (1.0 + bend) + 0.5 * pre * (1.0 - bend * bend) * inner)
    low = out.astype(BF16)
    if last:
        out_ref[...] = low
    else:
        for at in range(out_ref.shape[0]):
            out_ref[at] = low[:, at * LANES : (at + 1) * LANES]

    def squares(value):
        value = value.astype(F32)
        return jnp.sum(valid * (value * value), axis=0, keepdims=True)

    def lanes(value):
        return sum(value[:, i : i + LANES] for i in range(0, value.shape[1], LANES))

    @pl.when(step == 0)
    def _():
        stat_ref[...] = jnp.zeros_like(stat_ref)
        stat_ref[1:2, :] = lanes(squares(agg))
        stat_ref[4:5, :] = jnp.sum(jnp.broadcast_to(valid, (valid.shape[0], LANES)), axis=0, keepdims=True)

    stat_ref[0:1, :] += lanes(squares(input_ref[...]))
    stat_ref[2:3, :] += lanes(squares(out))
    stat_ref[3:4, :] += lanes(squares(low))


def dense_layer(agg, weight, bias, valid, inputs, last):
    chips, nodes, width = agg.shape
    full = weight.shape[1]
    steps = 4
    block = full // steps
    if last:
        out_spec = pl.BlockSpec((nodes, block), lambda f: (0, f))
        out_shape = jax.ShapeDtypeStruct((nodes, full), BF16)
        input_spec = pl.BlockSpec((nodes, LANES), lambda f: (0, 0))
    else:
        out_spec = pl.BlockSpec((chips // steps, nodes, width), lambda f: (f, 0, 0))
        out_shape = jax.ShapeDtypeStruct((chips, nodes, width), BF16)
        input_spec = pl.BlockSpec((nodes, block), lambda f: (0, f))
    return pl.pallas_call(
        functools.partial(dense_kernel, last),
        grid=(steps,),
        in_specs=[
            pl.BlockSpec((chips, nodes, width), lambda f: (0, 0, 0)),
            pl.BlockSpec((full, block), lambda f: (0, f)),
            pl.BlockSpec((1, block), lambda f: (0, f)),
            pl.BlockSpec((nodes, 1), lambda f: (0, 0)),
            input_spec,
        ],
        out_specs=[
            out_spec,
            pl.BlockSpec((nodes, block), lambda f: (0, f)),
            pl.BlockSpec((8, LANES), lambda f: (0, 0)),
        ],
        out_shape=[
            out_shape,
            jax.ShapeDtypeStruct((nodes, full), F32),
            jax.ShapeDtypeStruct((8, LANES), F32),
        ],
        cost_estimate=pl.CostEstimate(
            flops=2 * nodes * full * full, bytes_accessed=2 * full * full, transcendentals=nodes * full
        ),
    )(agg, weight, bias, valid, inputs)


def gradient_kernel(first, slope_ref, weight_ref, inverse_ref, *refs):
    (up_ref, extra_ref, other_ref), (pre_ref, agg_ref, sums_ref) = refs[:3], refs[3:]
    full = slope_ref.shape[1]
    inverse = inverse_ref[...]

    @pl.when(pl.program_id(0) == 0)
    def _():
        if first:
            for at in range(up_ref.shape[0]):
                here = slice(at * LANES, (at + 1) * LANES)
                up = up_ref[at].astype(F32) + 2.0 * extra_ref[at].astype(F32) * inverse
                pre_ref[:, here] = (up.T * slope_ref[:, here]).astype(BF16)
            pre_ref[:, full:] = jnp.zeros((pre_ref.shape[0], LANES), BF16)
        else:
            pre_ref[:, :full] = (up_ref[...].astype(F32) * slope_ref[...]).astype(BF16)
            one = jnp.sum(extra_ref[...], axis=1, keepdims=True)
            two = jnp.sum(other_ref[...], axis=1, keepdims=True)
            row = lax.broadcasted_iota(jnp.int32, (8, 1), 0)

            def pick(value, at, to):
                return jnp.where(row == to, jnp.sum(jnp.where(row == at, value, 0.0), axis=0, keepdims=True), 0.0)

            total = pick(one, 0, 0) + pick(one, 1, 1) + pick(one, 2, 2) + pick(one, 3, 3)
            total += pick(two, 1, 4) + pick(two, 2, 5) + pick(one * (1.0 / LANES), 4, 6)
            high = total.astype(BF16).astype(F32)
            both = jnp.concatenate([high, total - high], axis=0)
            rest = jnp.zeros((pre_ref.shape[0] - 16, LANES), BF16)
            pre_ref[:16, full:] = jnp.broadcast_to(both, (16, LANES)).astype(BF16)
            pre_ref[16:, full:] = rest

    grads = lax.dot_general(weight_ref[...], pre_ref[:, :full], NT, preferred_element_type=F32)
    low = grads.astype(BF16)
    sums = (low.astype(F32) * inverse).astype(BF16)
    for at in range(agg_ref.shape[0]):
        agg_ref[at] = low[at * LANES : (at + 1) * LANES]
        sums_ref[at] = sums[at * LANES : (at + 1) * LANES]


def gradient_layer(slope, weight, inverse, upstream, extra, other, first):
    nodes, full = slope.shape
    steps = 4
    block = full // steps
    chips = full // LANES
    whole = lambda value: pl.BlockSpec(value.shape, lambda k: (0,) * value.ndim)
    tiles = pl.BlockSpec((chips // steps, LANES, nodes), lambda k: (k, 0, 0))
    return pl.pallas_call(
        functools.partial(gradient_kernel, first),
        grid=(steps,),
        in_specs=[
            whole(slope),
            pl.BlockSpec((block, full), lambda k: (k, 0)),
            whole(inverse),
            whole(upstream),
            whole(extra),
            whole(other),
        ],
        out_specs=[pl.BlockSpec((nodes, full + LANES), lambda k: (0, 0)), tiles, tiles],
        out_shape=[
            jax.ShapeDtypeStruct((nodes, full + LANES), BF16),
            jax.ShapeDtypeStruct((chips, LANES, nodes), BF16),
            jax.ShapeDtypeStruct((chips, LANES, nodes), BF16),
        ],
        cost_estimate=pl.CostEstimate(
            flops=2 * nodes * full * full, bytes_accessed=2 * full * full, transcendentals=0
        ),
    )(slope, weight, inverse, upstream, extra, other)


def weight_kernel(row_ref, agg_ref, *refs):
    parts, (out_ref, left_ref) = refs[:10], refs[10:]
    row = row_ref[0]
    cols, piece_rows, full = out_ref.shape
    full -= LANES
    nodes = parts[0].shape[0]
    width = 2 * LANES
    for mask in range(8):
        for half in range(2):
            block = agg_ref[row ^ mask, half]
            left_ref[half * LANES : (half + 1) * LANES, mask * nodes : (mask + 1) * nodes] = block.T
    left_ref[width:, :] = jnp.ones((16, left_ref.shape[1]), BF16)
    order = [
        [parts[0]], [parts[5]], [parts[1]], [parts[6]], [parts[2]], [parts[7]],
        [parts[3], parts[4]], [parts[8], parts[9]],
    ]
    step = 512
    bias = []
    for at in range(0, full, step):
        right = jnp.concatenate([ref[:, at : at + step] for group in order for ref in group], axis=0)
        total = jnp.dot(left_ref[...], right, preferred_element_type=F32)
        for col in range(cols):
            out_ref[col, :, at : at + step] = total[col * piece_rows : (col + 1) * piece_rows].astype(BF16)
        bias.append(total[width : width + 8])
    bias = jnp.concatenate(bias, axis=1)
    mine = jnp.zeros((8, width), F32)
    for at in range(full // width):
        mine += jnp.where(row == at, bias[:, at * width : (at + 1) * width], 0.0)
    line = lax.broadcasted_iota(jnp.int32, (8, LANES), 0)
    mine = jnp.where(line % 2 == 0, mine[:, :LANES], mine[:, LANES:])
    mine_high = mine.astype(BF16).astype(F32)
    mine = jnp.where(line < 2, mine_high, jnp.where(line < 4, mine - mine_high, 0.0))
    stats = jnp.zeros((8, LANES), F32)
    for group in order:
        both = group[0][:16, full:].astype(F32)
        stats += both[:8] + both[8:]
    high = stats.astype(BF16).astype(F32)
    rest = jnp.zeros((piece_rows - 24, LANES), F32)
    extra = jnp.concatenate([mine, high, stats - high, rest], axis=0).astype(BF16)
    for col in range(cols):
        out_ref[col, :, full:] = extra


def weight_product(row, aggs, parts, cols):
    nodes, full = parts[0].shape
    full -= LANES
    rows = 2 * LANES // cols
    vmem = pl.BlockSpec(memory_space=pltpu.VMEM)
    return pl.pallas_call(
        weight_kernel,
        in_specs=[pl.BlockSpec(memory_space=pltpu.SMEM)] + [vmem] * 11,
        out_specs=vmem,
        out_shape=jax.ShapeDtypeStruct((cols, rows, full + LANES), BF16),
        scratch_shapes=[pltpu.VMEM((2 * LANES + 16, 8 * nodes), BF16)],
        cost_estimate=pl.CostEstimate(
            flops=2 * 8 * nodes * full * 2 * LANES, bytes_accessed=2 * 8 * nodes * full, transcendentals=0
        ),
    )(row, aggs, *parts)


def final_kernel(up_ref, agg_ref, inverse_ref, out_ref):
    inverse = inverse_ref[...]
    for at in range(up_ref.shape[0]):
        value = up_ref[at].astype(F32) + 2.0 * agg_ref[at].astype(F32) * inverse
        out_ref[:, at * LANES : (at + 1) * LANES] = value.T.astype(BF16)


def input_gradient(upstream, grad_agg, inverse):
    chips, width, nodes = upstream.shape
    vmem = pl.BlockSpec(memory_space=pltpu.VMEM)
    return pl.pallas_call(
        final_kernel,
        in_specs=[vmem] * 3,
        out_specs=vmem,
        out_shape=jax.ShapeDtypeStruct((nodes, chips * width), BF16),
    )(upstream, grad_agg, inverse)


def transposed(features, weight_one, bias_one, weight_two, bias_two, cotangent, neighbours, valid_mask):
    nodes, full = features.shape
    chip_rows, cols = lax.axis_size("ch"), lax.axis_size("col")
    chips = chip_rows * cols
    half = chips * nodes
    sources = 2 * half
    slots = neighbours.shape[1]
    core = lax.axis_index("core")
    col = lax.axis_index("col")
    row = 2 * lax.axis_index("ch") + core
    plane, every = ("ch", "core"), ("ch", "col")

    def swap(value):
        return lax.ppermute(value, "core", [(0, 1), (1, 0)])

    def across(value, mask):
        return lax.ppermute(value, "ch", [(i, i ^ mask) for i in range(chip_rows)])

    def exchange(value):
        return lax.all_to_all(value, every, 0, 0, tiled=True)

    lists = neighbours.reshape(1, -1, MXU)
    lists = jnp.broadcast_to(lists, (chip_rows,) + lists.shape[1:])
    lists = lax.all_to_all(lists, "ch", 0, 0, tiled=True).reshape(-1, MXU)
    live = lists >= 0
    node = jnp.maximum(lists, 0)
    owner, offset = node // nodes, node % nodes
    owner_row, owner_col = owner // cols, owner % cols
    place = ((owner_row // 2) * cols + owner_col) * nodes + offset
    place = jnp.where(owner_row % 2 == core, place, place + half)
    group_rows = MXU // slots
    line = lax.broadcasted_iota(jnp.int32, lists.shape, 1) // slots
    high = jnp.where(live, (place // MXU) * group_rows + line, -1)
    tile, wide_inverse = count_tiles(high, place % MXU, sources)

    own_lists = lax.dynamic_slice_in_dim(neighbours, col * nodes, nodes, 0)
    inverse = 1.0 / (jnp.sum(own_lists >= 0, axis=1).astype(F32) + 1.0)
    inverse = inverse.reshape(1, nodes)
    valid = valid_mask.astype(F32).reshape(nodes, 1)

    own = lax.all_to_all(features, every, 1, 0, tiled=True)
    agg_one = apply_forward(tile, own, swap(own), wide_inverse)
    agg_one = exchange(agg_one.reshape(chips, nodes, LANES))
    hidden, slope_one, stats_one = dense_layer(agg_one, weight_one, bias_one.reshape(1, -1), valid, features, False)
    own = exchange(hidden).reshape(half, LANES)
    agg_two = apply_forward(tile, own, swap(own), wide_inverse)
    agg_two = exchange(agg_two.reshape(chips, nodes, LANES))
    act, slope_two, stats_two = dense_layer(agg_two, weight_two, bias_two.reshape(1, -1), valid, features, True)

    def in_plane(aggs):
        aggs = aggs.reshape(2 * chip_rows, -1, nodes, LANES)
        return lax.all_to_all(aggs, plane, 0, 0, tiled=True)

    def gather_plane(value):
        by_x, by_y = across(value, 1), across(value, 2)
        cut = nodes // 2
        mine = [value, by_x, by_y, across(by_x[:cut], 2), across(by_y[cut:], 1)]
        return mine + [swap(part) for part in mine]

    def adjacency_backward(grads):
        grads = exchange(grads)
        more = swap(apply_backward(tile, grads, 1))
        return exchange(apply_backward(tile, grads, 0, more))

    def reduce_weight(aggs, grad_pre):
        parts = weight_product(row.reshape(1), in_plane(aggs), gather_plane(grad_pre), cols)
        parts = lax.all_to_all(parts, "col", 0, 0, tiled=True)
        total = jnp.sum(parts.astype(F32), axis=0)
        extra = total[:, full:]
        bias = (extra[0:2] + extra[2:4]).reshape(-1)
        count = full // (2 * chips)
        bias = lax.dynamic_slice_in_dim(bias, col * count, count, 0)
        return total[:, :full], bias, extra[8:16, 0] + extra[16:24, 0]

    grad_pre_two, grad_agg_two, sums_two = gradient_layer(
        slope_two, weight_two, inverse, cotangent, stats_one, stats_two, False
    )
    upstream = adjacency_backward(sums_two)
    weight_grad_two, bias_grad_two, stats = reduce_weight(agg_two, grad_pre_two)
    grad_pre_one, grad_agg_one, sums_one = gradient_layer(
        slope_one, weight_one, inverse, upstream, grad_agg_two, stats_one, True
    )
    grad_start = input_gradient(adjacency_backward(sums_one), grad_agg_one, inverse)
    weight_grad_one, bias_grad_one, _ = reduce_weight(agg_one, grad_pre_one)
    rms_stats = jnp.sqrt(stats[:6].reshape(2, 3) / (stats[6] * full) + 1e-06)
    return (act, grad_start, weight_grad_one, bias_grad_one, weight_grad_two, bias_grad_two, rms_stats)


def solution(mesh):
    rows, cols = mesh.devices.shape
    axes = ("ch", "core", "col")
    wide = Mesh(mesh.devices.reshape(rows // 2, 2, cols), axes)

    def program(features, *rest):
        nodes, full = features.shape
        slots = rest[5].shape[1]
        fits = (
            (rows, cols) == (8, 4)
            and nodes == rows * cols * LANES
            and full == rows * cols * 64
            and slots * nodes == MXU * MXU
        )
        split, over = (axes, wide) if fits else (("row", "col"), mesh)
        lists = ("ch", "core") if fits else "row"
        spread = P(split, None)
        return jax.shard_map(
            transposed if fits else general,
            mesh=over,
            in_specs=(spread, P(), P(), P(), P(), spread, P(lists, None), P(split)),
            out_specs=(spread, spread, spread, P(split), spread, P(split), P()),
            check_vma=False,
        )(features, *rest)

    return program
```

```python
import functools

import jax
import jax.numpy as jnp
from jax import lax
from jax.experimental import pallas as pl
from jax.experimental.pallas import tpu as pltpu
from jax.sharding import Mesh
from jax.sharding import PartitionSpec as P

BF16, F32 = jnp.bfloat16, jnp.float32
LANES = 128
MXU = 256
MIB = 1 << 20
NT = (((1,), (1,)), ((), ()))
GELU_C, GELU_A = 0.7978845608, 0.044715


def gelu_value(value):
    return jax.nn.gelu(value, approximate=True)


def source_parts(lists, per_dev, col_devs):
    live = lists >= 0
    safe = jnp.maximum(lists, 0)
    block = safe // per_dev
    return (live, block // col_devs, block % col_devs, safe % per_dev)


def block_tile(lists, usable, local_index, span):
    columns = jnp.arange(span, dtype=jnp.int32)[None, :]
    marked = jnp.where(usable, local_index, -1)
    total = jnp.zeros((lists.shape[0], span), jnp.float32)
    for slot in range(lists.shape[1]):
        total = total + (marked[:, slot : slot + 1] == columns).astype(jnp.float32)
    return total.astype(jnp.bfloat16)


def reduce_weights(grad_weight, grad_bias):
    return (
        lax.psum_scatter(grad_weight, ("row", "col"), scatter_dimension=0, tiled=True),
        lax.psum_scatter(grad_bias, ("row", "col"), scatter_dimension=0, tiled=True),
    )


def general(features, weight_one, bias_one, weight_two, bias_two, cotangent, neighbours, valid_mask):
    per_dev, width = features.shape
    row_devs = lax.axis_size("row")
    col_devs = lax.axis_size("col")
    col_pos = lax.axis_index("col")
    own_lists = lax.dynamic_slice_in_dim(neighbours, col_pos * per_dev, per_dev, 0)
    inverse = 1.0 / (jnp.sum(own_lists >= 0, axis=1).astype(jnp.float32) + 1.0)
    scaling = inverse[:, None]
    validity = valid_mask.astype(jnp.float32)[:, None]
    live, src_row, src_col, offset = source_parts(neighbours, per_dev, col_devs)
    front_tile = block_tile(
        neighbours, live & (src_col == col_pos), src_row * per_dev + offset, row_devs * per_dev
    )

    def forward_layer(inputs, weight, bias):
        gathered = lax.all_gather(inputs, "row", axis=0, tiled=True)
        partial_value = jnp.dot(front_tile, gathered, preferred_element_type=jnp.float32)
        summed = lax.psum_scatter(partial_value, "col", scatter_dimension=0, tiled=True)
        aggregate = ((summed + 2.0 * inputs.astype(jnp.float32)) * scaling).astype(jnp.bfloat16)
        preact = jnp.dot(aggregate, weight, preferred_element_type=jnp.float32) + bias
        return (aggregate, preact, validity * gelu_value(preact))

    agg_one, pre_one, out_one = forward_layer(features, weight_one, bias_one)
    hidden = out_one.astype(jnp.bfloat16)
    agg_two, pre_two, out_two = forward_layer(hidden, weight_two, bias_two)

    def squares(value):
        return jnp.sum(validity * jnp.square(value.astype(jnp.float32)))

    local_squares = jnp.stack(
        [
            squares(features),
            squares(agg_one),
            squares(out_one),
            squares(hidden),
            squares(agg_two),
            squares(out_two),
        ]
    ).reshape(2, 3)
    total_squares, total_valid = lax.psum((local_squares, jnp.sum(validity)), ("row", "col"))
    rms_stats = jnp.sqrt(total_squares / (total_valid * width) + 1e-06)

    def backward_layer(upstream, aggregate, preact, weight):
        grad_act = validity * upstream
        grad_pre = jax.vjp(gelu_value, preact)[1](grad_act)[0].astype(jnp.bfloat16)
        grad_weight = lax.dot_general(
            aggregate, grad_pre, (((0,), (0,)), ((), ())), preferred_element_type=jnp.float32
        )
        grad_bias = jnp.sum(grad_pre.astype(jnp.float32), axis=0)
        grad_low = lax.dot_general(
            grad_pre, weight, (((1,), (1,)), ((), ())), preferred_element_type=jnp.float32
        ).astype(jnp.bfloat16)
        grad_agg = lax.optimization_barrier(grad_low).astype(jnp.float32)
        grad_sum = (grad_agg * scaling).astype(jnp.bfloat16)
        grad_all = lax.all_gather(grad_sum, "col", axis=0, tiled=True)
        from_lists = lax.psum_scatter(
            lax.dot_general(
                front_tile, grad_all, (((0,), (0,)), ((), ())), preferred_element_type=jnp.float32
            ),
            "row",
            scatter_dimension=0,
            tiled=True,
        )
        return (from_lists + 2.0 * grad_agg * scaling, grad_weight, grad_bias)

    grad_hidden, weight_grad_two, bias_grad_two = backward_layer(
        cotangent.astype(jnp.float32), agg_two, pre_two, weight_two
    )
    weight_grad_two, bias_grad_two = reduce_weights(weight_grad_two, bias_grad_two)
    grad_start, weight_grad_one, bias_grad_one = backward_layer(
        grad_hidden, agg_one, pre_one, weight_one
    )
    weight_grad_one, bias_grad_one = reduce_weights(weight_grad_one, bias_grad_one)
    return (
        out_two.astype(jnp.bfloat16),
        grad_start.astype(jnp.bfloat16),
        weight_grad_one,
        bias_grad_one,
        weight_grad_two,
        bias_grad_two,
        rms_stats,
    )


IN_VMEM = pl.BlockSpec(memory_space=pltpu.VMEM)
IN_SMEM = pl.BlockSpec(memory_space=pltpu.SMEM)
IN_ANY = pl.BlockSpec(memory_space=pl.ANY)
COUNT = jnp.float8_e4m3fn
PARAMS = pltpu.CompilerParams(vmem_limit_bytes=62 * MIB)


def cost(flops, read, transcendentals=0):
    return pl.CostEstimate(flops=flops, bytes_accessed=read, transcendentals=transcendentals)


def lanes(at, size=LANES):
    return slice(at * size, (at + 1) * size)


def fetch(source, target, semaphore):
    copy = pltpu.make_async_copy(source, target, semaphore)
    copy.start()
    return copy


def stream(source, blocks, target, semaphores):
    copies = [fetch(source.at[block], target.at[block], semaphores.at[i]) for i, block in enumerate(blocks)]

    def arrivals():
        for block, copy in zip(blocks, copies, strict=True):
            copy.wait()
            yield target[block]

    return arrivals()


def buffer(shape, blocks, dtype=BF16):
    return [pltpu.VMEM(shape, dtype), pltpu.SemaphoreType.DMA((blocks,))]


def like(value):
    return [pltpu.VMEM(value.shape, value.dtype), pltpu.SemaphoreType.DMA]


class Results:
    def __init__(self, semaphores):
        self.semaphores, self.copies = semaphores, []

    def send(self, source, target):
        self.copies.append(fetch(source, target, self.semaphores.at[len(self.copies)]))

    def wait(self):
        for copy in self.copies:
            copy.wait()


def column_blocks(size, step):
    return [(slice(None), slice(at, at + step)) for at in range(0, size, step)]


def row_blocks(size, step):
    return [(slice(at, at + step), slice(None)) for at in range(0, size, step)]


def tile_kernel(turn, nodes, cols, place_ref, lists_ref, tile_ref):
    masks, lines, width = lists_ref.shape
    groups = 8
    rows = LANES // groups
    chip_row, core = place_ref[0] // 2, place_ref[0] % 2
    step = pl.program_id(0)
    per_chip = lines // groups
    mask = chip_row ^ (step // per_chip)
    lists = lists_ref[mask, pl.ds(pl.multiple_of(step % per_chip * groups, groups), groups), :]
    node_bits, col_bits = nodes.bit_length() - 1, cols.bit_length() - 1
    owner_row = lists >> (node_bits + col_bits)
    within = lists & (nodes * cols - 1)
    place = ((owner_row >> 1) << (node_bits + col_bits)) + within
    live = lists >= 0
    if turn:
        half = masks * cols * nodes
        place = jnp.where((owner_row & 1) == core, place, place + half)
    else:
        live &= (owner_row & 1) == core
    line = lax.broadcasted_iota(jnp.int32, lists.shape, 1) // rows
    highs = jnp.where(live, (place // MXU) * rows + line, -1)
    lows = place % MXU
    blocks = (tile_ref.shape[0] if turn else tile_ref.shape[1]) // MXU
    high_place = lax.broadcasted_iota(jnp.int32, (blocks * rows, width), 0)
    low_place = lax.broadcasted_iota(jnp.int32, (MXU, width), 0)
    pieces = []
    for group in range(groups):
        high = (high_place == highs[group : group + 1, :]).astype(F32).astype(BF16)
        low = (low_place == lows[group : group + 1, :]).astype(F32).astype(BF16)
        counts = lax.dot_general(high, low, NT, preferred_element_type=F32)
        pieces.append(counts.astype(BF16))
    for block in range(blocks):
        column = jnp.concatenate([piece[block * rows : (block + 1) * rows] for piece in pieces], axis=0)
        if turn:
            for side in range(2):
                turned = column[:, lanes(side)].T
                tile_ref[lanes(2 * block + side), :] = turned.astype(COUNT)
        else:
            tile_ref[:, lanes(block, MXU)] = column.astype(COUNT)


def count_tile(at, lists, nodes, cols, turn):
    masks, lines, width = lists.shape
    rows = masks * lines * 16
    half = masks * cols * nodes
    shape = (2 * half, rows) if turn else (rows, half)
    block = (2 * half, LANES) if turn else (LANES, half)
    return pl.pallas_call(
        functools.partial(tile_kernel, turn, nodes, cols),
        grid=(rows // LANES,),
        in_specs=[IN_SMEM, pl.BlockSpec(lists.shape, lambda i: (0, 0, 0))],
        out_specs=pl.BlockSpec(block, (lambda i: (0, i)) if turn else (lambda i: (i, 0))),
        out_shape=jax.ShapeDtypeStruct(shape, COUNT),
        compiler_params=PARAMS,
        cost_estimate=cost(4 * rows * shape[0 if turn else 1] * 2 * MXU, rows * half),
    )(at, lists)


def adjacency_kernel(forward, tiles, own_ref, other_ref, *refs):
    tile_refs, refs = refs[:tiles], refs[-10 - tiles :]
    out_ref, left_ref, total_ref, own, own_sem, other, other_sem = refs[:7]
    buffers, (semaphores, out, out_sems) = refs[7 : 7 + tiles], refs[7 + tiles :]
    chips, width = own_ref.shape[0], LANES
    half = chips * width
    copies = [fetch(own_ref, own, own_sem), fetch(other_ref, other, other_sem)]
    chunks, arrivals = [], []
    for ref, target in zip(tile_refs, buffers, strict=True):
        for at in range(0, ref.shape[0], half):
            here = slice(at, at + half)
            arrivals.append(fetch(ref.at[here], target.at[here], semaphores.at[len(chunks)]))
            chunks.append(target.at[here])
    for copy in copies:
        copy.wait()
    for at in range(chips):
        left_ref[:width, lanes(at)] = own[at].T if forward else own[at]
        left_ref[:width, lanes(chips + at)] = other[at].T if forward else other[at]
    if forward:
        left_ref[width:, :] = jnp.ones((left_ref.shape[0] - width, left_ref.shape[1]), BF16)
    for block, (copy, counts) in enumerate(zip(arrivals, chunks, strict=True)):
        copy.wait()
        part = jnp.dot(left_ref[:, lanes(block, half)], counts[...].astype(BF16), preferred_element_type=F32)
        if block == 0:
            total_ref[...] = part
        else:
            total_ref[...] += part
    results = Results(out_sems)
    group = chips // out_sems.shape[0]
    for at in range(chips):
        here = lanes(at)
        if forward:
            inverse = 1.0 / (total_ref[width : width + 1, here] + 1.0)
            value = (total_ref[:width, here] + 2.0 * left_ref[:width, here].astype(F32)) * inverse
            out[at] = value.astype(BF16).T
        else:
            out[at] = total_ref[:, here].astype(BF16)
        if (at + 1) % group == 0:
            done = slice(at + 1 - group, at + 1)
            results.send(out.at[done], out_ref.at[done])
    results.wait()


def apply_adjacency(tiles, own, other, forward, *after):
    sources, half = sum(tile.shape[0] for tile in tiles), tiles[0].shape[1]
    rows = LANES + (16 if forward else 0)
    scratch = [pltpu.VMEM((rows, sources), BF16), pltpu.VMEM((rows, half), F32)] + like(own) + like(other)
    scratch += [pltpu.VMEM(tile.shape, COUNT) for tile in tiles] + [pltpu.SemaphoreType.DMA((sources // half,))]
    return pl.pallas_call(
        functools.partial(adjacency_kernel, forward, len(tiles)),
        in_specs=[IN_ANY] * (2 + len(tiles) + len(after)),
        out_specs=IN_ANY,
        out_shape=jax.ShapeDtypeStruct(own.shape, BF16),
        scratch_shapes=scratch + buffer(own.shape, 4),
        compiler_params=PARAMS,
        cost_estimate=cost(2 * half * sources * LANES, half * sources),
    )(own, other, *tiles, *after)


def gelu_parts(pre, valid):
    square = pre * pre
    bend = jnp.tanh(GELU_C * (pre + GELU_A * (square * pre)))
    inner = GELU_C * (1.0 + 3.0 * GELU_A * square)
    slope = 0.5 * (1.0 + bend) + 0.5 * pre * (1.0 - bend * bend) * inner
    return valid * (0.5 * pre * (1.0 + bend)), valid * slope


def lane_squares(value, valid):
    value = value.astype(F32)
    value = jnp.sum(valid * (value * value), axis=0, keepdims=True)
    return sum(value[:, lanes(i)] for i in range(value.shape[1] // LANES))


def send_pieces(at_ref, agg_blocks, pieces, piece_refs, results):
    chip_row = at_ref[0] // 2
    blocks = agg_blocks.shape[0] // len(piece_refs)
    for mask, ref in enumerate(piece_refs):
        for part in range(blocks):
            pieces[mask, :, lanes(part)] = agg_blocks[(chip_row ^ mask) * blocks + part]
        results.send(pieces.at[mask], ref)


def first_kernel(at_ref, agg_ref, weight_ref, bias_ref, valid_ref, input_ref, *refs):
    out_ref, slope_ref, stat_ref = refs[-17:-14]
    piece_refs = refs[-14:-10]
    agg_blocks, agg_sem, inputs, input_sem, weight_buffer, semaphores = refs[-10:-4]
    out, slopes, pieces, out_sems = refs[-4:]
    chips, nodes, width = agg_ref.shape
    full = weight_ref.shape[1]
    step = full // semaphores.shape[0]
    copies = [fetch(agg_ref, agg_blocks, agg_sem)]
    weights = stream(weight_ref, column_blocks(full, step), weight_buffer, semaphores)
    copies.append(fetch(input_ref, inputs, input_sem))
    results = Results(out_sems)
    valid = valid_ref[...]
    copies[0].wait()
    agg = jnp.concatenate([agg_blocks[i] for i in range(chips)], axis=1)
    send_pieces(at_ref, agg_blocks, pieces, piece_refs, results)
    none = jnp.zeros((1, LANES), F32)
    of_agg, of_input, of_out, of_low = lane_squares(agg, valid), none, none, none
    for block, weight in enumerate(weights):
        here = lanes(block, step)
        pre = jnp.dot(agg, weight, preferred_element_type=F32) + bias_ref[:, here]
        value, slopes[:, here] = gelu_parts(pre, valid)
        low = value.astype(BF16)
        of_out += lane_squares(value, valid)
        of_low += lane_squares(low, valid)
        if block == 0:
            copies[1].wait()
        of_input += lane_squares(inputs[:, here], valid)
        blocks = lanes(block, step // LANES)
        for part in range(step // LANES):
            out[blocks.start + part] = low[:, lanes(part)]
        results.send(out.at[blocks], out_ref.at[blocks])
        results.send(slopes.at[:, here], slope_ref.at[:, here])
    count = jnp.sum(jnp.broadcast_to(valid, (nodes, LANES)), axis=0, keepdims=True) * (1.0 / LANES)
    stat_ref[...] = jnp.concatenate([of_input, of_agg, of_out, of_low, count, none, none, none], axis=0)
    results.wait()


def piece_shapes(agg, chip_rows):
    chips, nodes, width = agg.shape
    return [jax.ShapeDtypeStruct((nodes, chips * width // chip_rows), BF16)] * chip_rows


def first_layer(at, agg, weight, bias, valid, inputs, chip_rows, *after):
    chips, nodes, width = agg.shape
    full = weight.shape[1]
    pieces = piece_shapes(agg, chip_rows)
    steps = 2
    return pl.pallas_call(
        first_kernel,
        in_specs=[IN_SMEM, IN_ANY, IN_ANY, IN_VMEM, IN_VMEM, IN_ANY] + [IN_ANY] * len(after),
        out_specs=[IN_ANY, IN_ANY, IN_VMEM] + [IN_ANY] * chip_rows,
        out_shape=[
            jax.ShapeDtypeStruct(agg.shape, BF16),
            jax.ShapeDtypeStruct((nodes, full), F32),
            jax.ShapeDtypeStruct((8, LANES), F32),
        ]
        + pieces,
        scratch_shapes=like(agg)
        + like(inputs)
        + buffer(weight.shape, steps)
        + [
            pltpu.VMEM(agg.shape, BF16),
            pltpu.VMEM((nodes, full), F32),
            pltpu.VMEM((chip_rows,) + pieces[0].shape, BF16),
            pltpu.SemaphoreType.DMA((chip_rows + 2 * steps,)),
        ],
        compiler_params=PARAMS,
        cost_estimate=cost(2 * nodes * full * full, 2 * full * full, nodes * full),
    )(at, agg, weight, bias, valid, inputs, *after)


def gradient_blocks(weight, blocks, turned, inverse, outs, refs, results):
    low = jnp.dot(weight, turned[...], preferred_element_type=F32).astype(BF16)
    sums = (low.astype(F32) * inverse).astype(BF16)
    for value, out, ref in zip((sums, low), outs, refs, strict=True):
        for part in range(weight.shape[0] // LANES):
            out[blocks.start + part] = value[lanes(part)]
        results.send(out.at[blocks], ref.at[blocks])


def second_kernel(
    at_ref, agg_ref, weight_ref, bias_ref, valid_ref, cotangent_ref, inverse_ref, stat_ref, *refs
):
    act_ref, pre_ref, sums_ref, grad_agg_ref = refs[-21:-17]
    piece_refs = refs[-17:-13]
    agg_blocks, agg_sem, cotangent, cotangent_sem, weight_buffer, semaphores = refs[-13:-7]
    act, pres, turned, sums, grad_agg, pieces, out_sems = refs[-7:]
    chips, nodes, width = agg_ref.shape
    full = weight_ref.shape[1]
    step = full // semaphores.shape[0]
    copies = [fetch(agg_ref, agg_blocks, agg_sem)]
    weights = stream(weight_ref, column_blocks(full, step), weight_buffer, semaphores)
    copies.append(fetch(cotangent_ref, cotangent, cotangent_sem))
    results = Results(out_sems)
    valid, inverse = valid_ref[...], inverse_ref[...]
    copies[0].wait()
    agg = jnp.concatenate([agg_blocks[i] for i in range(chips)], axis=1)
    send_pieces(at_ref, agg_blocks, pieces, piece_refs, results)
    of_agg, of_out = lane_squares(agg, valid), jnp.zeros((1, LANES), F32)
    for block, weight in enumerate(weights):
        here = lanes(block, step)
        pre = jnp.dot(agg, weight, preferred_element_type=F32) + bias_ref[:, here]
        value, slope = gelu_parts(pre, valid)
        of_out += lane_squares(value, valid)
        act[:, here] = value.astype(BF16)
        results.send(act.at[:, here], act_ref.at[:, here])
        if block == 0:
            copies[1].wait()
        grad_pre = (cotangent[:, here].astype(F32) * slope).astype(BF16)
        pres[:, here] = grad_pre
        for part in range(step // LANES):
            turned[block * step + part * LANES : block * step + (part + 1) * LANES, :] = grad_pre[:, lanes(part)].T
    stat = stat_ref[...]
    rows = [stat[:4], of_agg, of_out, stat[4:5], jnp.zeros((1, LANES), F32)]
    total = jnp.sum(jnp.concatenate(rows, axis=0), axis=1, keepdims=True)
    high = total.astype(BF16).astype(F32)
    both = jnp.concatenate([high, total - high], axis=0)
    pres[:16, full:] = jnp.broadcast_to(both, (16, LANES)).astype(BF16)
    pres[16:, full:] = jnp.zeros((nodes - 16, LANES), BF16)
    results.send(pres, pre_ref)
    step = full // 4
    for block in range(4):
        gradient_blocks(
            weight_buffer[lanes(block, step), :], lanes(block, step // LANES), turned, inverse,
            (sums, grad_agg), (sums_ref, grad_agg_ref), results,
        )
    results.wait()


def second_layer(at, agg, weight, bias, valid, cotangent, inverse, stats, chip_rows, *after):
    chips, nodes, width = agg.shape
    full = weight.shape[1]
    blocks = jax.ShapeDtypeStruct((chips, width, nodes), BF16)
    pieces = piece_shapes(agg, chip_rows)
    steps = 2
    return pl.pallas_call(
        second_kernel,
        in_specs=[IN_SMEM, IN_ANY, IN_ANY, IN_VMEM, IN_VMEM, IN_ANY, IN_VMEM, IN_VMEM] + [IN_ANY] * len(after),
        out_specs=[IN_ANY] * (4 + chip_rows),
        out_shape=[
            jax.ShapeDtypeStruct((nodes, full), BF16),
            jax.ShapeDtypeStruct((nodes, full + LANES), BF16),
            blocks,
            blocks,
        ]
        + pieces,
        scratch_shapes=like(agg)
        + like(cotangent)
        + buffer(weight.shape, steps)
        + [
            pltpu.VMEM((nodes, full), BF16),
            pltpu.VMEM((nodes, full + LANES), BF16),
            pltpu.VMEM((full, nodes), BF16),
            pltpu.VMEM(blocks.shape, BF16),
            pltpu.VMEM(blocks.shape, BF16),
            pltpu.VMEM((chip_rows,) + pieces[0].shape, BF16),
            pltpu.SemaphoreType.DMA((chip_rows + steps + 1 + 8,)),
        ],
        compiler_params=PARAMS,
        cost_estimate=cost(4 * nodes * full * full, 2 * full * full, nodes * full),
    )(at, agg, weight, bias, valid, cotangent, inverse, stats, *after)


def back_kernel(slope_ref, weight_ref, inverse_ref, up_ref, extra_ref, *refs):
    pre_ref, sums_ref, agg_ref, slope, slope_sem, up, up_sem, extra, extra_sem = refs[-16:-7]
    weight_buffer, semaphores, pres, turned, sums, grad_agg, out_sems = refs[-7:]
    nodes, full = slope_ref.shape
    step = full // semaphores.shape[0]
    copies = [fetch(up_ref, up, up_sem), fetch(extra_ref, extra, extra_sem), fetch(slope_ref, slope, slope_sem)]
    weights = stream(weight_ref, row_blocks(full, step), weight_buffer, semaphores)
    results = Results(out_sems)
    inverse = inverse_ref[...]
    for copy in copies:
        copy.wait()
    for at in range(up_ref.shape[0]):
        value = up[at].astype(F32) + 2.0 * extra[at].astype(F32) * inverse
        grad_pre = (value.T * slope[:, lanes(at)]).astype(BF16)
        pres[:, lanes(at)] = grad_pre
        turned[lanes(at), :] = grad_pre.T
    pres[:, full:] = jnp.zeros((nodes, LANES), BF16)
    results.send(pres, pre_ref)
    for block, weight in enumerate(weights):
        gradient_blocks(
            weight, lanes(block, step // LANES), turned, inverse, (sums, grad_agg), (sums_ref, agg_ref), results
        )
    results.wait()


def first_layer_back(slope, weight, inverse, upstream, extra, *after):
    nodes, full = slope.shape
    blocks = jax.ShapeDtypeStruct(upstream.shape, BF16)
    steps = 1
    return pl.pallas_call(
        back_kernel,
        in_specs=[IN_ANY, IN_ANY, IN_VMEM, IN_ANY, IN_ANY] + [IN_ANY] * len(after),
        out_specs=[IN_ANY] * 3,
        out_shape=[jax.ShapeDtypeStruct((nodes, full + LANES), BF16), blocks, blocks],
        scratch_shapes=like(slope)
        + like(upstream)
        + like(extra)
        + buffer(weight.shape, steps)
        + [
            pltpu.VMEM((nodes, full + LANES), BF16),
            pltpu.VMEM((full, nodes), BF16),
            pltpu.VMEM(blocks.shape, BF16),
            pltpu.VMEM(blocks.shape, BF16),
            pltpu.SemaphoreType.DMA((1 + 2 * steps,)),
        ],
        compiler_params=PARAMS,
        cost_estimate=cost(2 * nodes * full * full, 2 * full * full),
    )(slope, weight, inverse, upstream, extra, *after)


def left_factor(at_ref, lefts, left_parts, left_sem, left_ref):
    nodes = lefts[0].shape[0]
    width = left_parts.shape[2]
    mine = pl.ds(pl.multiple_of(at_ref[0] % 2 * width, width), width)
    copies = [fetch(ref.at[:, mine], left_parts.at[i], left_sem.at[i]) for i, ref in enumerate(lefts)]

    def finish():
        for i, copy in enumerate(copies):
            copy.wait()
            left_ref[:width, lanes(i, nodes)] = left_parts[i].T
        left_ref[width:, :] = jnp.ones((left_ref.shape[0] - width, left_ref.shape[1]), BF16)

    return finish


def products(at_ref, left_ref, right, copies, width, use):
    bias = jnp.zeros((8, width), F32)
    step = right.shape[1] // len(copies)
    for block, group in enumerate(copies):
        for copy in group:
            copy.wait()
        here = lanes(block, step)
        total = jnp.dot(left_ref[...], right[:, here], preferred_element_type=F32)
        use(here, total)
        for part in range(step // width):
            one = block * (step // width) + part
            bias += jnp.where(at_ref[0] == one, total[width : width + 8, lanes(part, width)], 0.0)
    return bias


def second_weight_kernel(at_ref, *refs):
    lefts, right_ref = refs[:8], refs[8]
    out_ref, side_ref, left_parts, left_sem, right, right_sems, stat_parts, stat_sems, left_ref = refs[-9:]
    nodes, width = left_parts.shape[1:]
    full = right.shape[1]
    finish = left_factor(at_ref, lefts, left_parts, left_sem, left_ref)
    rows = [pl.ds(pl.multiple_of((at_ref[0] ^ i) * nodes, nodes), nodes) for i in range(8)]
    steps = right_sems.shape[0]
    copies = [
        [
            fetch(
                right_ref.at[source, lanes(block, full // steps)],
                right.at[lanes(i, nodes), lanes(block, full // steps)],
                right_sems.at[block, i],
            )
            for i, source in enumerate(rows)
        ]
        for block in range(steps)
    ]
    stat_copies = [
        fetch(right_ref.at[lanes(i, nodes), slice(full, full + LANES)], stat_parts.at[i], stat_sems.at[i])
        for i in range(8)
    ]
    finish()

    def use(here, total):
        out_ref[:, here] = total[:width].astype(BF16)

    side_ref[:8, :] = products(at_ref, left_ref, right, copies, width, use)
    stats = jnp.zeros((8, LANES), F32)
    for i, copy in enumerate(stat_copies):
        copy.wait()
        both = stat_parts[i, :16].astype(F32)
        stats += both[:8] + both[8:]
    side_ref[8:, :LANES] = stats
    side_ref[8:, LANES:] = jnp.zeros((8, width - LANES), F32)


def second_weight(at, lefts, right):
    rows, full = right.shape
    full -= LANES
    nodes, width = rows // 8, lefts[0].shape[1] // 2
    return pl.pallas_call(
        second_weight_kernel,
        in_specs=[IN_SMEM] + [IN_ANY] * 9,
        out_specs=[IN_VMEM] * 2,
        out_shape=[jax.ShapeDtypeStruct((width, full), BF16), jax.ShapeDtypeStruct((16, width), F32)],
        scratch_shapes=[
            pltpu.VMEM((8, nodes, width), BF16),
            pltpu.SemaphoreType.DMA((8,)),
            pltpu.VMEM((rows, full), BF16),
            pltpu.SemaphoreType.DMA((2, 8)),
            pltpu.VMEM((8, nodes, LANES), BF16),
            pltpu.SemaphoreType.DMA((8,)),
            pltpu.VMEM((width + 16, rows), BF16),
        ],
        compiler_params=PARAMS,
        cost_estimate=cost(2 * rows * full * width, 4 * rows * full),
    )(at, *lefts, right)


def first_weight_kernel(at_ref, side_ref, *refs):
    lefts, rights, outs = refs[:8], refs[8:-9], refs[-9:-5]
    left_parts, left_sem, right, right_sems, left_ref = refs[-5:]
    col = at_ref[1]
    piece_rows, full = outs[0].shape
    full -= LANES
    nodes, width = left_parts.shape[1:]
    finish = left_factor(at_ref, lefts, left_parts, left_sem, left_ref)
    steps = right_sems.shape[0]
    starts = [sum(ref.shape[0] for ref in rights[:i]) for i in range(len(rights))]
    copies = [
        [
            fetch(
                ref.at[:, lanes(block, full // steps)],
                right.at[slice(start, start + ref.shape[0]), lanes(block, full // steps)],
                right_sems.at[block, i],
            )
            for i, (ref, start) in enumerate(zip(rights, starts, strict=True))
        ]
        for block in range(steps)
    ]
    finish()

    def use(here, total):
        for mask, ref in enumerate(outs):
            value = total[:piece_rows]
            for piece in range(1, len(outs)):
                value = jnp.where(col ^ mask == piece, total[piece * piece_rows : (piece + 1) * piece_rows], value)
            ref[:, here] = value.astype(BF16)

    bias_one = products(at_ref, left_ref, right, copies, width, use)
    bias_two, stats = side_ref[:8, :], side_ref[8:, :LANES]
    stats_high = stats.astype(BF16).astype(F32)
    rest = jnp.zeros((piece_rows - 24, LANES), F32)
    line = lax.broadcasted_iota(jnp.int32, (8, LANES), 0)
    for mask, ref in enumerate(outs):
        piece = col ^ mask
        rows = []
        for bias in (bias_one, bias_two):
            one = jnp.where(piece >= 2, bias[:, LANES:], bias[:, :LANES])
            one = jnp.where(piece % 2 == 1, pltpu.roll(one, LANES // 2, 1), one)
            high = one.astype(BF16).astype(F32)
            rows += [high, one - high]
        first = jnp.zeros((8, LANES), F32)
        for i, row in enumerate(rows):
            first = jnp.where(line == i, row, first)
        ref[:, full:] = jnp.concatenate([first, stats_high, stats - stats_high, rest], axis=0).astype(BF16)


def first_weight(at, side, lefts, rights, cols):
    nodes, full = lefts[0].shape[0], rights[0].shape[1]
    full -= LANES
    width = lefts[0].shape[1] // 2
    return pl.pallas_call(
        first_weight_kernel,
        in_specs=[IN_SMEM, IN_VMEM] + [IN_ANY] * (8 + len(rights)),
        out_specs=[IN_VMEM] * cols,
        out_shape=[jax.ShapeDtypeStruct((width // cols, full + LANES), BF16)] * cols,
        scratch_shapes=[
            pltpu.VMEM((8, nodes, width), BF16),
            pltpu.SemaphoreType.DMA((8,)),
            pltpu.VMEM((8 * nodes, full), BF16),
            pltpu.SemaphoreType.DMA((2, len(rights))),
            pltpu.VMEM((width + 16, 8 * nodes), BF16),
        ],
        compiler_params=PARAMS,
        cost_estimate=cost(2 * 8 * nodes * full * width, 4 * 8 * nodes * full),
    )(at, side, *lefts, *rights)


def sum_kernel(*refs):
    parts, (out_ref, bias_ref, stat_ref) = refs[:-3], refs[-3:]
    full = out_ref.shape[1]
    step = 512
    for at in range(0, full, step):
        here = slice(at, at + step)
        out_ref[:, here] = sum([part[:, here].astype(F32) for part in parts[1:]], parts[0][:, here].astype(F32))
    extra = sum([part[:, full:].astype(F32) for part in parts[1:]], parts[0][:, full:].astype(F32))
    bias_ref[0:1, :] = extra[0:1] + extra[1:2]
    bias_ref[1:2, :] = extra[2:3] + extra[3:4]
    stat_ref[...] = extra[8:16] + extra[16:24]


def sum_pieces(parts):
    rows, full = parts[0].shape
    full -= LANES
    return pl.pallas_call(
        sum_kernel,
        in_specs=[IN_VMEM] * len(parts),
        out_specs=[IN_VMEM] * 3,
        out_shape=[
            jax.ShapeDtypeStruct((rows, full), F32),
            jax.ShapeDtypeStruct((2, LANES), F32),
            jax.ShapeDtypeStruct((8, LANES), F32),
        ],
        compiler_params=PARAMS,
    )(*parts)


def final_kernel(up_ref, agg_ref, inverse_ref, out_ref):
    inverse = inverse_ref[...]
    for at in range(up_ref.shape[0]):
        value = up_ref[at].astype(F32) + 2.0 * agg_ref[at].astype(F32) * inverse
        out_ref[:, lanes(at)] = value.T.astype(BF16)


def input_gradient(upstream, grad_agg, inverse):
    chips, width, nodes = upstream.shape
    return pl.pallas_call(
        final_kernel,
        in_specs=[IN_VMEM] * 3,
        out_specs=IN_VMEM,
        out_shape=jax.ShapeDtypeStruct((nodes, chips * width), BF16),
        compiler_params=PARAMS,
    )(upstream, grad_agg, inverse)


def transposed(features, weight_one, bias_one, weight_two, bias_two, cotangent, neighbours, valid_mask):
    nodes, full = features.shape
    chip_rows, cols = lax.axis_size("ch"), lax.axis_size("col")
    chips = chip_rows * cols
    core = lax.axis_index("core")
    col = lax.axis_index("col")
    row = (2 * lax.axis_index("ch") + core).reshape(1)
    every = ("ch", "col")

    def swap(value):
        return lax.ppermute(value, "core", [(0, 1), (1, 0)])

    def across(value, mask):
        return lax.ppermute(value, "ch", [(i, i ^ mask) for i in range(chip_rows)])

    def exchange(value):
        return lax.all_to_all(value, every, 0, 0, tiled=True)

    at = jnp.concatenate([row, col.reshape(1)])

    lists = neighbours.reshape(-1, MXU)
    lists = jnp.stack([lists] + [across(lists, mask) for mask in range(1, chip_rows)])
    own = exchange(jnp.transpose(features.reshape(nodes, chips, LANES), (1, 0, 2)))
    turned = count_tile(at, lists, nodes, cols, True)
    tile_own = count_tile(at, lists, nodes, cols, False)
    tile_other = count_tile(at, swap(lists), nodes, cols, False)

    own_lists = lax.dynamic_slice_in_dim(neighbours, col * nodes, nodes, 0)
    inverse = 1.0 / (jnp.sum(own_lists >= 0, axis=1).astype(F32) + 1.0)
    inverse = inverse.reshape(1, nodes)
    valid = valid_mask.astype(F32).reshape(nodes, 1)

    def to_plane(parts):
        return [parts[0]] + [across(parts[mask], mask) for mask in range(1, chip_rows)]

    def both_cores(parts):
        return [part for one in parts for part in (one, swap(one))]

    def over_cols(parts):
        return [parts[0]] + [
            lax.ppermute(parts[mask], "col", [(i, i ^ mask) for i in range(cols)]) for mask in range(1, cols)
        ]

    def exchange_beside(value, *others):
        return lax.optimization_barrier((exchange(value), *others))

    own, turned = lax.optimization_barrier((own, turned))
    agg_one = exchange(apply_adjacency([turned], own, swap(own), True))
    agg_one, tile_own = lax.optimization_barrier((agg_one, tile_own))
    hidden, slope_one, stats_one, *pieces_one = first_layer(
        at, agg_one, weight_one, bias_one.reshape(1, -1), valid, features, chip_rows
    )
    own, tile_other = exchange_beside(hidden, tile_other)
    agg_two = apply_adjacency([turned], own, swap(own), True)
    agg_two, *pieces_one = exchange_beside(agg_two, *to_plane(pieces_one))
    act, grad_pre_two, sums_two, grad_agg_two, *pieces_two = second_layer(
        at, agg_two, weight_two, bias_two.reshape(1, -1), valid, cotangent, inverse, stats_one, chip_rows
    )
    all_two = lax.all_gather(grad_pre_two, ("ch", "core"), axis=0, tiled=True)
    own, *pieces_two = exchange_beside(sums_two, *to_plane(pieces_two))
    upstream = apply_adjacency([tile_own, tile_other], own, swap(own), False)
    weight_grad_two, side = second_weight(at, both_cores(pieces_two), all_two)
    upstream, weight_grad_two, side = exchange_beside(upstream, weight_grad_two, side)
    weight_grad_two = lax.psum_scatter(weight_grad_two, "col", scatter_dimension=0, tiled=True).astype(F32)
    grad_pre_one, sums_one, grad_agg_one = first_layer_back(slope_one, weight_one, inverse, upstream, grad_agg_two)
    own, by_x, by_y = exchange_beside(sums_one, across(grad_pre_one, 1), across(grad_pre_one, 2))
    cut = nodes // 2
    plane_one = [grad_pre_one, by_x, by_y, across(by_x[:cut], 2), across(by_y[cut:], 1)]
    grad_start = exchange(apply_adjacency([tile_own, tile_other], own, swap(own), False))
    grad_start = input_gradient(grad_start, grad_agg_one, inverse)
    rights = both_cores(plane_one[:3]) + plane_one[3:] + [swap(part) for part in plane_one[3:]]
    parts_one = first_weight(at, side, both_cores(pieces_one), rights, cols)
    weight_grad_one, biases, stats = sum_pieces(over_cols(parts_one))
    count = full // (2 * chips)
    bias_grad_two, bias_grad_one = biases[1, :count], biases[0, :count]
    stats = stats[:, 0]
    rms_stats = jnp.sqrt(stats[:6].reshape(2, 3) / (stats[6] * full) + 1e-06)
    return (act, grad_start, weight_grad_one, bias_grad_one, weight_grad_two, bias_grad_two, rms_stats)


def solution(mesh):
    rows, cols = mesh.devices.shape
    axes = ("ch", "core", "col")
    wide = Mesh(mesh.devices.reshape(rows // 2, 2, cols), axes)

    def program(features, *rest):
        nodes, full = features.shape
        slots = rest[5].shape[1]
        fits = (
            (rows, cols) == (8, 4)
            and nodes == rows * cols * LANES
            and full == rows * cols * 64
            and slots * nodes == MXU * MXU
            and slots == 16
        )
        split, over = (axes, wide) if fits else (("row", "col"), mesh)
        lists = ("ch", "core") if fits else "row"
        spread = P(split, None)
        return jax.shard_map(
            transposed if fits else general,
            mesh=over,
            in_specs=(spread, P(), P(), P(), P(), spread, P(lists, None), P(split)),
            out_specs=(spread, spread, spread, P(split), spread, P(split), P()),
            check_vma=False,
        )(features, *rest)

    return program
```

```python
import functools

import jax
import jax.numpy as jnp
from jax import lax
from jax.experimental import pallas as pl
from jax.experimental.pallas import tpu as pltpu
from jax.sharding import Mesh
from jax.sharding import PartitionSpec as P

BF16, F32 = jnp.bfloat16, jnp.float32
LANES = 128
MXU = 256
MIB = 1 << 20
NT = (((1,), (1,)), ((), ()))
GELU_C, GELU_A = 0.7978845608, 0.044715


def gelu_value(value):
    return jax.nn.gelu(value, approximate=True)


def source_parts(lists, per_dev, col_devs):
    live = lists >= 0
    safe = jnp.maximum(lists, 0)
    block = safe // per_dev
    return (live, block // col_devs, block % col_devs, safe % per_dev)


def block_tile(lists, usable, local_index, span):
    columns = jnp.arange(span, dtype=jnp.int32)[None, :]
    marked = jnp.where(usable, local_index, -1)
    total = jnp.zeros((lists.shape[0], span), jnp.float32)
    for slot in range(lists.shape[1]):
        total = total + (marked[:, slot : slot + 1] == columns).astype(jnp.float32)
    return total.astype(jnp.bfloat16)


def reduce_weights(grad_weight, grad_bias):
    return (
        lax.psum_scatter(grad_weight, ("row", "col"), scatter_dimension=0, tiled=True),
        lax.psum_scatter(grad_bias, ("row", "col"), scatter_dimension=0, tiled=True),
    )


def general(features, weight_one, bias_one, weight_two, bias_two, cotangent, neighbours, valid_mask):
    per_dev, width = features.shape
    row_devs = lax.axis_size("row")
    col_devs = lax.axis_size("col")
    col_pos = lax.axis_index("col")
    own_lists = lax.dynamic_slice_in_dim(neighbours, col_pos * per_dev, per_dev, 0)
    inverse = 1.0 / (jnp.sum(own_lists >= 0, axis=1).astype(jnp.float32) + 1.0)
    scaling = inverse[:, None]
    validity = valid_mask.astype(jnp.float32)[:, None]
    live, src_row, src_col, offset = source_parts(neighbours, per_dev, col_devs)
    front_tile = block_tile(
        neighbours, live & (src_col == col_pos), src_row * per_dev + offset, row_devs * per_dev
    )

    def forward_layer(inputs, weight, bias):
        gathered = lax.all_gather(inputs, "row", axis=0, tiled=True)
        partial_value = jnp.dot(front_tile, gathered, preferred_element_type=jnp.float32)
        summed = lax.psum_scatter(partial_value, "col", scatter_dimension=0, tiled=True)
        aggregate = ((summed + 2.0 * inputs.astype(jnp.float32)) * scaling).astype(jnp.bfloat16)
        preact = jnp.dot(aggregate, weight, preferred_element_type=jnp.float32) + bias
        return (aggregate, preact, validity * gelu_value(preact))

    agg_one, pre_one, out_one = forward_layer(features, weight_one, bias_one)
    hidden = out_one.astype(jnp.bfloat16)
    agg_two, pre_two, out_two = forward_layer(hidden, weight_two, bias_two)

    def squares(value):
        return jnp.sum(validity * jnp.square(value.astype(jnp.float32)))

    local_squares = jnp.stack(
        [
            squares(features),
            squares(agg_one),
            squares(out_one),
            squares(hidden),
            squares(agg_two),
            squares(out_two),
        ]
    ).reshape(2, 3)
    total_squares, total_valid = lax.psum((local_squares, jnp.sum(validity)), ("row", "col"))
    rms_stats = jnp.sqrt(total_squares / (total_valid * width) + 1e-06)

    def backward_layer(upstream, aggregate, preact, weight):
        grad_act = validity * upstream
        grad_pre = jax.vjp(gelu_value, preact)[1](grad_act)[0].astype(jnp.bfloat16)
        grad_weight = lax.dot_general(
            aggregate, grad_pre, (((0,), (0,)), ((), ())), preferred_element_type=jnp.float32
        )
        grad_bias = jnp.sum(grad_pre.astype(jnp.float32), axis=0)
        grad_low = lax.dot_general(
            grad_pre, weight, (((1,), (1,)), ((), ())), preferred_element_type=jnp.float32
        ).astype(jnp.bfloat16)
        grad_agg = lax.optimization_barrier(grad_low).astype(jnp.float32)
        grad_sum = (grad_agg * scaling).astype(jnp.bfloat16)
        grad_all = lax.all_gather(grad_sum, "col", axis=0, tiled=True)
        from_lists = lax.psum_scatter(
            lax.dot_general(
                front_tile, grad_all, (((0,), (0,)), ((), ())), preferred_element_type=jnp.float32
            ),
            "row",
            scatter_dimension=0,
            tiled=True,
        )
        return (from_lists + 2.0 * grad_agg * scaling, grad_weight, grad_bias)

    grad_hidden, weight_grad_two, bias_grad_two = backward_layer(
        cotangent.astype(jnp.float32), agg_two, pre_two, weight_two
    )
    weight_grad_two, bias_grad_two = reduce_weights(weight_grad_two, bias_grad_two)
    grad_start, weight_grad_one, bias_grad_one = backward_layer(
        grad_hidden, agg_one, pre_one, weight_one
    )
    weight_grad_one, bias_grad_one = reduce_weights(weight_grad_one, bias_grad_one)
    return (
        out_two.astype(jnp.bfloat16),
        grad_start.astype(jnp.bfloat16),
        weight_grad_one,
        bias_grad_one,
        weight_grad_two,
        bias_grad_two,
        rms_stats,
    )


IN_VMEM = pl.BlockSpec(memory_space=pltpu.VMEM)
IN_SMEM = pl.BlockSpec(memory_space=pltpu.SMEM)
IN_ANY = pl.BlockSpec(memory_space=pl.ANY)
COUNT = jnp.float8_e4m3fn
PARAMS = pltpu.CompilerParams(vmem_limit_bytes=64 * MIB - 192 * 1024)


def cost(flops, read, transcendentals=0):
    return pl.CostEstimate(flops=flops, bytes_accessed=read, transcendentals=transcendentals)


def lanes(at, size=LANES):
    return slice(at * size, (at + 1) * size)


def fetch(source, target, semaphore):
    copy = pltpu.make_async_copy(source, target, semaphore)
    copy.start()
    return copy


def stream(source, blocks, target, semaphores):
    copies = [fetch(source.at[block], target.at[block], semaphores.at[i]) for i, block in enumerate(blocks)]

    def arrivals():
        for block, copy in zip(blocks, copies, strict=True):
            copy.wait()
            yield target[block]

    return arrivals()


def buffer(shape, blocks, dtype=BF16):
    return [pltpu.VMEM(shape, dtype), pltpu.SemaphoreType.DMA((blocks,))]


def like(value):
    return [pltpu.VMEM(value.shape, value.dtype), pltpu.SemaphoreType.DMA]


class Results:
    def __init__(self, semaphores):
        self.semaphores, self.copies = semaphores, []

    def send(self, source, target):
        self.copies.append(fetch(source, target, self.semaphores.at[len(self.copies)]))

    def wait(self):
        for copy in self.copies:
            copy.wait()


def column_blocks(size, step):
    return [(slice(None), slice(at, at + step)) for at in range(0, size, step)]


def row_blocks(size, step):
    return [(slice(at, at + step), slice(None)) for at in range(0, size, step)]


def tile_kernel(turn, nodes, cols, place_ref, lists_ref, tile_ref, tile, semaphores):
    masks, lines, width = lists_ref.shape
    groups = 8
    rows = LANES // groups
    chip_row, core = place_ref[0] // 2, place_ref[0] % 2
    per_chip = lines // groups
    blocks = (tile.shape[0] if turn else tile.shape[1]) // MXU
    node_bits, col_bits = nodes.bit_length() - 1, cols.bit_length() - 1

    def one_block(step, carry):
        mask = chip_row ^ (step // per_chip)
        lists = lists_ref[mask, pl.ds(pl.multiple_of(step % per_chip * groups, groups), groups), :]
        owner_row = lists >> (node_bits + col_bits)
        within = lists & (nodes * cols - 1)
        place = ((owner_row >> 1) << (node_bits + col_bits)) + within
        live = lists >= 0
        if turn:
            half = masks * cols * nodes
            place = jnp.where((owner_row & 1) == core, place, place + half)
        else:
            live &= (owner_row & 1) == core
        line = lax.broadcasted_iota(jnp.int32, lists.shape, 1) // rows
        highs = jnp.where(live, (place // MXU) * rows + line, -1)
        lows = place % MXU
        high_place = lax.broadcasted_iota(jnp.int32, (blocks * rows, width), 0)
        low_place = lax.broadcasted_iota(jnp.int32, (MXU, width), 0)
        pieces = []
        for group in range(groups):
            high = (high_place == highs[group : group + 1, :]).astype(F32).astype(BF16)
            low = (low_place == lows[group : group + 1, :]).astype(F32).astype(BF16)
            counts = lax.dot_general(high, low, NT, preferred_element_type=F32)
            pieces.append(counts.astype(BF16))
        here = pl.ds(pl.multiple_of(step * LANES, LANES), LANES)
        for block in range(blocks):
            column = jnp.concatenate([piece[block * rows : (block + 1) * rows] for piece in pieces], axis=0)
            if turn:
                for side in range(2):
                    turned = column[:, lanes(side)].T
                    tile[lanes(2 * block + side), here] = turned.astype(COUNT)
            else:
                tile[here, lanes(block, MXU)] = column.astype(COUNT)
        return carry

    results = Results(semaphores)
    steps = masks * per_chip
    chunks = semaphores.shape[0]
    size = steps // chunks
    for chunk in range(chunks):
        lax.fori_loop(chunk * size, (chunk + 1) * size, one_block, 0)
        done = lanes(chunk, size * LANES)
        part = (slice(None), done) if turn else (done, slice(None))
        results.send(tile.at[part], tile_ref.at[part])
    results.wait()


def count_tile(at, lists, nodes, cols, turn):
    masks, lines, width = lists.shape
    rows = masks * lines * 16
    half = masks * cols * nodes
    shape = (2 * half, rows) if turn else (rows, half)
    return pl.pallas_call(
        functools.partial(tile_kernel, turn, nodes, cols),
        in_specs=[IN_SMEM, IN_VMEM],
        out_specs=IN_ANY,
        out_shape=jax.ShapeDtypeStruct(shape, COUNT),
        scratch_shapes=buffer(shape, 4, COUNT),
        compiler_params=PARAMS,
        cost_estimate=cost(4 * rows * shape[0 if turn else 1] * 2 * MXU, rows * half),
    )(at, lists)


def adjacency_kernel(forward, tiles, own_ref, other_ref, *refs):
    tile_refs, refs = refs[:tiles], refs[-10 - tiles :]
    out_ref, left_ref, total_ref, own, own_sem, other, other_sem = refs[:7]
    buffers, (semaphores, out, out_sems) = refs[7 : 7 + tiles], refs[7 + tiles :]
    chips, width = out.shape[0], LANES
    half = chips * width
    flat = len(own_ref.shape) == 2
    copies = [fetch(own_ref, own, own_sem), fetch(other_ref, other, other_sem)]
    chunks, arrivals = [], []
    for ref, target in zip(tile_refs, buffers, strict=True):
        for at in range(0, ref.shape[0], half):
            here = slice(at, at + half)
            arrivals.append(fetch(ref.at[here], target.at[here], semaphores.at[len(chunks)]))
            chunks.append(target.at[here])
    for copy in copies:
        copy.wait()
    for at in range(chips):
        mine, others = (own[lanes(at), :], other[lanes(at), :]) if flat else (own[at], other[at])
        left_ref[:width, lanes(at)] = mine.T if forward else mine
        left_ref[:width, lanes(chips + at)] = others.T if forward else others
    if forward:
        left_ref[width:, :] = jnp.ones((left_ref.shape[0] - width, left_ref.shape[1]), BF16)
    for block, (copy, counts) in enumerate(zip(arrivals, chunks, strict=True)):
        copy.wait()
        part = jnp.dot(left_ref[:, lanes(block, half)], counts[...].astype(BF16), preferred_element_type=F32)
        if block == 0:
            total_ref[...] = part
        else:
            total_ref[...] += part
    results = Results(out_sems)
    group = chips // out_sems.shape[0]
    for at in range(chips):
        here = lanes(at)
        if forward:
            inverse = 1.0 / (total_ref[width : width + 1, here] + 1.0)
            value = (total_ref[:width, here] + 2.0 * left_ref[:width, here].astype(F32)) * inverse
            out[at] = value.astype(BF16).T
        else:
            out[at] = total_ref[:, here].astype(BF16)
        if (at + 1) % group == 0:
            done = slice(at + 1 - group, at + 1)
            results.send(out.at[done], out_ref.at[done])
    results.wait()


def apply_adjacency(tiles, own, other, forward, *after):
    sources, half = sum(tile.shape[0] for tile in tiles), tiles[0].shape[1]
    rows = LANES + (16 if forward else 0)
    blocks = (half // LANES, LANES, LANES)
    scratch = [pltpu.VMEM((rows, sources), BF16), pltpu.VMEM((rows, half), F32)] + like(own) + like(other)
    scratch += [pltpu.VMEM(tile.shape, COUNT) for tile in tiles] + [pltpu.SemaphoreType.DMA((sources // half,))]
    return pl.pallas_call(
        functools.partial(adjacency_kernel, forward, len(tiles)),
        in_specs=[IN_ANY] * (2 + len(tiles) + len(after)),
        out_specs=IN_ANY,
        out_shape=jax.ShapeDtypeStruct(blocks, BF16),
        scratch_shapes=scratch + buffer(blocks, 4),
        compiler_params=PARAMS,
        cost_estimate=cost(2 * half * sources * LANES, half * sources),
    )(own, other, *tiles, *after)


def gelu_parts(pre, valid):
    square = pre * pre
    bend = jnp.tanh(GELU_C * (pre + GELU_A * (square * pre)))
    inner = GELU_C * (1.0 + 3.0 * GELU_A * square)
    slope = 0.5 * (1.0 + bend) + 0.5 * pre * (1.0 - bend * bend) * inner
    return valid * (0.5 * pre * (1.0 + bend)), valid * slope


def lane_squares(value, valid):
    value = value.astype(F32)
    value = jnp.sum(valid * (value * value), axis=0, keepdims=True)
    return sum(value[:, lanes(i)] for i in range(value.shape[1] // LANES))


def send_pieces(at_ref, agg_blocks, pieces, piece_refs, results):
    chip_row = at_ref[0] // 2
    blocks = agg_blocks.shape[0] // len(piece_refs)
    for mask, ref in enumerate(piece_refs):
        for part in range(blocks):
            pieces[mask, :, lanes(part)] = agg_blocks[(chip_row ^ mask) * blocks + part]
        results.send(pieces.at[mask], ref)


def first_kernel(at_ref, agg_ref, weight_ref, bias_ref, valid_ref, input_ref, *refs):
    out_ref, slope_ref, stat_ref = refs[-17:-14]
    piece_refs = refs[-14:-10]
    agg_blocks, agg_sem, inputs, input_sem, weight_buffer, semaphores = refs[-10:-4]
    out, slopes, pieces, out_sems = refs[-4:]
    chips, nodes, width = agg_ref.shape
    full = weight_ref.shape[1]
    step = full // semaphores.shape[0]
    copies = [fetch(agg_ref, agg_blocks, agg_sem)]
    weights = stream(weight_ref, column_blocks(full, step), weight_buffer, semaphores)
    copies.append(fetch(input_ref, inputs, input_sem))
    results = Results(out_sems)
    valid = valid_ref[...]
    copies[0].wait()
    agg = jnp.concatenate([agg_blocks[i] for i in range(chips)], axis=1)
    send_pieces(at_ref, agg_blocks, pieces, piece_refs, results)
    none = jnp.zeros((1, LANES), F32)
    of_agg, of_input, of_out, of_low = lane_squares(agg, valid), none, none, none
    for block, weight in enumerate(weights):
        here = lanes(block, step)
        pre = jnp.dot(agg, weight, preferred_element_type=F32) + bias_ref[:, here]
        value, slopes[:, here] = gelu_parts(pre, valid)
        low = value.astype(BF16)
        of_out += lane_squares(value, valid)
        of_low += lane_squares(low, valid)
        if block == 0:
            copies[1].wait()
        of_input += lane_squares(inputs[:, here], valid)
        blocks = lanes(block, step // LANES)
        for part in range(step // LANES):
            out[blocks.start + part] = low[:, lanes(part)]
        results.send(out.at[blocks], out_ref.at[blocks])
        results.send(slopes.at[:, here], slope_ref.at[:, here])
    count = jnp.sum(jnp.broadcast_to(valid, (nodes, LANES)), axis=0, keepdims=True) * (1.0 / LANES)
    stat_ref[...] = jnp.concatenate([of_input, of_agg, of_out, of_low, count, none, none, none], axis=0)
    results.wait()


def piece_shapes(agg, chip_rows):
    chips, nodes, width = agg.shape
    return [jax.ShapeDtypeStruct((nodes, chips * width // chip_rows), BF16)] * chip_rows


def first_layer(at, agg, weight, bias, valid, inputs, chip_rows, *after):
    chips, nodes, width = agg.shape
    full = weight.shape[1]
    pieces = piece_shapes(agg, chip_rows)
    steps = 2
    return pl.pallas_call(
        first_kernel,
        in_specs=[IN_SMEM, IN_ANY, IN_ANY, IN_VMEM, IN_VMEM, IN_ANY] + [IN_ANY] * len(after),
        out_specs=[IN_ANY, IN_ANY, IN_VMEM] + [IN_ANY] * chip_rows,
        out_shape=[
            jax.ShapeDtypeStruct(agg.shape, BF16),
            jax.ShapeDtypeStruct((nodes, full), F32),
            jax.ShapeDtypeStruct((8, LANES), F32),
        ]
        + pieces,
        scratch_shapes=like(agg)
        + like(inputs)
        + buffer(weight.shape, steps)
        + [
            pltpu.VMEM(agg.shape, BF16),
            pltpu.VMEM((nodes, full), F32),
            pltpu.VMEM((chip_rows,) + pieces[0].shape, BF16),
            pltpu.SemaphoreType.DMA((chip_rows + 2 * steps,)),
        ],
        compiler_params=PARAMS,
        cost_estimate=cost(2 * nodes * full * full, 2 * full * full, nodes * full),
    )(at, agg, weight, bias, valid, inputs, *after)


def gradient_blocks(weight, blocks, turned, inverse, outs, refs, results):
    low = jnp.dot(weight, turned[...], preferred_element_type=F32).astype(BF16)
    sums = (low.astype(F32) * inverse).astype(BF16)
    for value, out, ref in zip((sums, low), outs, refs, strict=True):
        for part in range(weight.shape[0] // LANES):
            out[blocks.start + part] = value[lanes(part)]
        results.send(out.at[blocks], ref.at[blocks])


def second_kernel(
    at_ref, agg_ref, weight_ref, bias_ref, valid_ref, cotangent_ref, inverse_ref, stat_ref, *refs
):
    act_ref, pre_ref, sums_ref, grad_agg_ref = refs[-21:-17]
    piece_refs = refs[-17:-13]
    agg_blocks, agg_sem, cotangent, cotangent_sem, weight_buffer, semaphores = refs[-13:-7]
    act, pres, turned, sums, grad_agg, pieces, out_sems = refs[-7:]
    chips, nodes, width = agg_ref.shape
    full = weight_ref.shape[1]
    step = full // semaphores.shape[0]
    copies = [fetch(agg_ref, agg_blocks, agg_sem)]
    weights = stream(weight_ref, column_blocks(full, step), weight_buffer, semaphores)
    copies.append(fetch(cotangent_ref, cotangent, cotangent_sem))
    results = Results(out_sems)
    valid, inverse = valid_ref[...], inverse_ref[...]
    copies[0].wait()
    agg = jnp.concatenate([agg_blocks[i] for i in range(chips)], axis=1)
    send_pieces(at_ref, agg_blocks, pieces, piece_refs, results)
    of_agg, of_out = lane_squares(agg, valid), jnp.zeros((1, LANES), F32)
    for block, weight in enumerate(weights):
        here = lanes(block, step)
        pre = jnp.dot(agg, weight, preferred_element_type=F32) + bias_ref[:, here]
        value, slope = gelu_parts(pre, valid)
        of_out += lane_squares(value, valid)
        act[:, here] = value.astype(BF16)
        results.send(act.at[:, here], act_ref.at[:, here])
        if block == 0:
            copies[1].wait()
        grad_pre = (cotangent[:, here].astype(F32) * slope).astype(BF16)
        pres[:, here] = grad_pre
        for part in range(step // LANES):
            turned[block * step + part * LANES : block * step + (part + 1) * LANES, :] = grad_pre[:, lanes(part)].T
    stat = stat_ref[...]
    rows = [stat[:4], of_agg, of_out, stat[4:5], jnp.zeros((1, LANES), F32)]
    total = jnp.sum(jnp.concatenate(rows, axis=0), axis=1, keepdims=True)
    high = total.astype(BF16).astype(F32)
    both = jnp.concatenate([high, total - high], axis=0)
    pres[:16, full:] = jnp.broadcast_to(both, (16, LANES)).astype(BF16)
    pres[16:, full:] = jnp.zeros((nodes - 16, LANES), BF16)
    results.send(pres, pre_ref)
    step = full // 4
    for block in range(4):
        gradient_blocks(
            weight_buffer[lanes(block, step), :], lanes(block, step // LANES), turned, inverse,
            (sums, grad_agg), (sums_ref, grad_agg_ref), results,
        )
    results.wait()


def second_layer(at, agg, weight, bias, valid, cotangent, inverse, stats, chip_rows, *after):
    chips, nodes, width = agg.shape
    full = weight.shape[1]
    blocks = jax.ShapeDtypeStruct((chips, width, nodes), BF16)
    pieces = piece_shapes(agg, chip_rows)
    steps = 2
    return pl.pallas_call(
        second_kernel,
        in_specs=[IN_SMEM, IN_ANY, IN_ANY, IN_VMEM, IN_VMEM, IN_ANY, IN_VMEM, IN_VMEM] + [IN_ANY] * len(after),
        out_specs=[IN_ANY] * (4 + chip_rows),
        out_shape=[
            jax.ShapeDtypeStruct((nodes, full), BF16),
            jax.ShapeDtypeStruct((nodes, full + LANES), BF16),
            blocks,
            blocks,
        ]
        + pieces,
        scratch_shapes=like(agg)
        + like(cotangent)
        + buffer(weight.shape, steps)
        + [
            pltpu.VMEM((nodes, full), BF16),
            pltpu.VMEM((nodes, full + LANES), BF16),
            pltpu.VMEM((full, nodes), BF16),
            pltpu.VMEM(blocks.shape, BF16),
            pltpu.VMEM(blocks.shape, BF16),
            pltpu.VMEM((chip_rows,) + pieces[0].shape, BF16),
            pltpu.SemaphoreType.DMA((chip_rows + steps + 1 + 8,)),
        ],
        compiler_params=PARAMS,
        cost_estimate=cost(4 * nodes * full * full, 2 * full * full, nodes * full),
    )(at, agg, weight, bias, valid, cotangent, inverse, stats, *after)


def back_kernel(slope_ref, weight_ref, inverse_ref, up_ref, extra_ref, *refs):
    pre_ref, sums_ref, agg_ref, slope, slope_sem, up, up_sem, extra, extra_sem = refs[-16:-7]
    weight_buffer, semaphores, pres, turned, sums, grad_agg, out_sems = refs[-7:]
    nodes, full = slope_ref.shape
    step = full // semaphores.shape[0]
    copies = [fetch(up_ref, up, up_sem), fetch(extra_ref, extra, extra_sem), fetch(slope_ref, slope, slope_sem)]
    weights = stream(weight_ref, row_blocks(full, step), weight_buffer, semaphores)
    results = Results(out_sems)
    inverse = inverse_ref[...]
    for copy in copies:
        copy.wait()
    for at in range(up_ref.shape[0]):
        value = up[at].astype(F32) + 2.0 * extra[at].astype(F32) * inverse
        grad_pre = (value.T * slope[:, lanes(at)]).astype(BF16)
        pres[:, lanes(at)] = grad_pre
        turned[lanes(at), :] = grad_pre.T
    pres[:, full:] = jnp.zeros((nodes, LANES), BF16)
    results.send(pres, pre_ref)
    for block, weight in enumerate(weights):
        gradient_blocks(
            weight, lanes(block, step // LANES), turned, inverse, (sums, grad_agg), (sums_ref, agg_ref), results
        )
    results.wait()


def first_layer_back(slope, weight, inverse, upstream, extra, *after):
    nodes, full = slope.shape
    blocks = jax.ShapeDtypeStruct(upstream.shape, BF16)
    steps = 1
    return pl.pallas_call(
        back_kernel,
        in_specs=[IN_ANY, IN_ANY, IN_VMEM, IN_ANY, IN_ANY] + [IN_ANY] * len(after),
        out_specs=[IN_ANY] * 3,
        out_shape=[jax.ShapeDtypeStruct((nodes, full + LANES), BF16), blocks, blocks],
        scratch_shapes=like(slope)
        + like(upstream)
        + like(extra)
        + buffer(weight.shape, steps)
        + [
            pltpu.VMEM((nodes, full + LANES), BF16),
            pltpu.VMEM((full, nodes), BF16),
            pltpu.VMEM(blocks.shape, BF16),
            pltpu.VMEM(blocks.shape, BF16),
            pltpu.SemaphoreType.DMA((1 + 2 * steps,)),
        ],
        compiler_params=PARAMS,
        cost_estimate=cost(2 * nodes * full * full, 2 * full * full),
    )(slope, weight, inverse, upstream, extra, *after)


def left_factor(at_ref, lefts, left_parts, left_sem, left_ref):
    nodes = lefts[0].shape[0]
    width = left_parts.shape[2]
    mine = pl.ds(pl.multiple_of(at_ref[0] % 2 * width, width), width)
    copies = [fetch(ref.at[:, mine], left_parts.at[i], left_sem.at[i]) for i, ref in enumerate(lefts)]

    def finish():
        for i, copy in enumerate(copies):
            copy.wait()
            left_ref[:width, lanes(i, nodes)] = left_parts[i].T
        left_ref[width:, :] = jnp.ones((left_ref.shape[0] - width, left_ref.shape[1]), BF16)

    return finish


def products(at_ref, left_ref, right, copies, width, use):
    bias = jnp.zeros((8, width), F32)
    step = right.shape[1] // len(copies)
    for block, group in enumerate(copies):
        for copy in group:
            copy.wait()
        here = lanes(block, step)
        total = jnp.dot(left_ref[...], right[:, here], preferred_element_type=F32)
        use(here, total)
        for part in range(step // width):
            one = block * (step // width) + part
            bias += jnp.where(at_ref[0] == one, total[width : width + 8, lanes(part, width)], 0.0)
    return bias


def small_sums(bias, stats, rows):
    high, stats_high = bias.astype(BF16).astype(F32), stats.astype(BF16).astype(F32)
    line = lax.broadcasted_iota(jnp.int32, (8, LANES), 0)
    first = jnp.where(line == 0, high, jnp.where(line == 1, bias - high, 0.0))
    rest = jnp.zeros((rows - 24, LANES), F32)
    return jnp.concatenate([first, stats_high, stats - stats_high, rest], axis=0).astype(BF16)


def read_small(extra):
    return extra[0:1] + extra[1:2], extra[8:16] + extra[16:24]


def weight_kernel(masks, at_ref, *refs):
    lefts, rights, outs = refs[:8], refs[8 : -7 - len(masks)], refs[-7 - len(masks) : -7]
    left_parts, left_sem, right, right_sems, stat_parts, stat_sems, left_ref = refs[-7:]
    col = at_ref[1]
    full = outs[0].shape[1] - LANES
    piece_rows = outs[0].shape[0] // len(masks[0])
    pieces = sum(len(group) for group in masks)
    nodes, width = left_parts.shape[1:]
    finish = left_factor(at_ref, lefts, left_parts, left_sem, left_ref)
    steps = right_sems.shape[0]
    starts = [sum(ref.shape[0] for ref in rights[:i]) for i in range(len(rights))]
    copies = [
        [
            fetch(
                ref.at[:, lanes(block, full // steps)],
                right.at[slice(start, start + ref.shape[0]), lanes(block, full // steps)],
                right_sems.at[block, i],
            )
            for i, (ref, start) in enumerate(zip(rights, starts, strict=True))
        ]
        for block in range(steps)
    ]
    firsts = [ref for ref, start in zip(rights, starts, strict=True) if start % nodes == 0]
    stat_copies = [
        fetch(ref.at[:16, slice(full, full + LANES)], stat_parts.at[i], stat_sems.at[i])
        for i, ref in enumerate(firsts)
    ]
    finish()

    def use(here, total):
        for group, ref in zip(masks, outs, strict=True):
            for at, mask in enumerate(group):
                value = total[:piece_rows]
                for piece in range(1, pieces):
                    value = jnp.where(col ^ mask == piece, total[lanes(piece, piece_rows)], value)
                ref[lanes(at, piece_rows), here] = value.astype(BF16)

    bias = products(at_ref, left_ref, right, copies, width, use)
    stats = jnp.zeros((8, LANES), F32)
    for i, copy in enumerate(stat_copies):
        copy.wait()
        both = stat_parts[i].astype(F32)
        stats += both[:8] + both[8:]
    for group, ref in zip(masks, outs, strict=True):
        for at, mask in enumerate(group):
            piece = col ^ mask
            one = jnp.where(piece >= 2, bias[:, LANES:], bias[:, :LANES])
            one = jnp.where(piece % 2 == 1, pltpu.roll(one, LANES // 2, 1), one)
            ref[lanes(at, piece_rows), full:] = small_sums(one, stats, piece_rows)


def weight_product(at, lefts, rights, masks):
    nodes, full = lefts[0].shape[0], rights[0].shape[1]
    full -= LANES
    width = lefts[0].shape[1] // 2
    rows = width // sum(len(group) for group in masks)
    return pl.pallas_call(
        functools.partial(weight_kernel, masks),
        in_specs=[IN_SMEM] + [IN_ANY] * (8 + len(rights)),
        out_specs=[IN_VMEM] * len(masks),
        out_shape=[jax.ShapeDtypeStruct((rows * len(group), full + LANES), BF16) for group in masks],
        scratch_shapes=[
            pltpu.VMEM((8, nodes, width), BF16),
            pltpu.SemaphoreType.DMA((8,)),
            pltpu.VMEM((8 * nodes, full), BF16),
            pltpu.SemaphoreType.DMA((2, len(rights))),
            pltpu.VMEM((8, 16, LANES), BF16),
            pltpu.SemaphoreType.DMA((8,)),
            pltpu.VMEM((width + 16, 8 * nodes), BF16),
        ],
        compiler_params=PARAMS,
        cost_estimate=cost(2 * 8 * nodes * full * width, 4 * 8 * nodes * full),
    )(at, *lefts, *rights)


def pair_kernel(one_ref, two_ref, out_ref):
    rows, full = out_ref.shape
    full -= LANES
    step = 512
    for at in range(0, full, step):
        here = slice(at, at + step)
        out_ref[:, here] = (one_ref[rows:, here].astype(F32) + two_ref[rows:, here].astype(F32)).astype(BF16)
    bias, stats = read_small(one_ref[rows:, full:].astype(F32) + two_ref[rows:, full:].astype(F32))
    out_ref[:, full:] = small_sums(bias, stats, rows)


def pair_sum(one, two):
    return pl.pallas_call(
        pair_kernel,
        in_specs=[IN_VMEM] * 2,
        out_specs=IN_VMEM,
        out_shape=jax.ShapeDtypeStruct((one.shape[0] // 2, one.shape[1]), BF16),
        compiler_params=PARAMS,
    )(one, two)


def sum_kernel(*refs):
    parts, (out_ref, bias_ref, rms_ref) = refs[:-3], refs[-3:]
    rows, full = out_ref.shape
    count = bias_ref.shape[1]

    def total(here):
        return sum([part[:rows, here].astype(F32) for part in parts[1:]], parts[0][:rows, here].astype(F32))

    step = 512
    for at in range(0, full, step):
        out_ref[:, at : at + step] = total(slice(at, at + step))
    bias, stats = read_small(total(slice(full, full + LANES)))
    bias_ref[...] = bias[:, :count]
    rms = jnp.sqrt(stats / jnp.maximum(stats[6:7] * full, 1.0) + 1e-06)
    row = lax.broadcasted_iota(jnp.int32, rms_ref.shape, 0)
    place = 3 * row + lax.broadcasted_iota(jnp.int32, rms_ref.shape, 1)
    value = jnp.zeros(rms_ref.shape, F32)
    for at in range(6):
        value = jnp.where(place == at, rms[at : at + 1, :3], value)
    rms_ref[...] = value


def sum_pieces(parts):
    rows, full = parts[-1].shape
    full -= LANES
    return pl.pallas_call(
        sum_kernel,
        in_specs=[IN_VMEM] * len(parts),
        out_specs=[IN_VMEM] * 3,
        out_shape=[
            jax.ShapeDtypeStruct((rows, full), F32),
            jax.ShapeDtypeStruct((1, rows), F32),
            jax.ShapeDtypeStruct((2, 3), F32),
        ],
        compiler_params=PARAMS,
    )(*parts)


def final_kernel(up_ref, agg_ref, inverse_ref, out_ref):
    inverse = inverse_ref[...]
    for at in range(up_ref.shape[0]):
        value = up_ref[at].astype(F32) + 2.0 * agg_ref[at].astype(F32) * inverse
        out_ref[:, lanes(at)] = value.T.astype(BF16)


def input_gradient(upstream, grad_agg, inverse):
    chips, width, nodes = upstream.shape
    return pl.pallas_call(
        final_kernel,
        in_specs=[IN_VMEM] * 3,
        out_specs=IN_VMEM,
        out_shape=jax.ShapeDtypeStruct((nodes, chips * width), BF16),
        compiler_params=PARAMS,
    )(upstream, grad_agg, inverse)


def transposed(features, weight_one, bias_one, weight_two, bias_two, cotangent, neighbours, valid_mask):
    nodes, full = features.shape
    chip_rows, cols = lax.axis_size("ch"), lax.axis_size("col")
    chips = chip_rows * cols
    core = lax.axis_index("core")
    col = lax.axis_index("col")
    row = (2 * lax.axis_index("ch") + core).reshape(1)
    every = ("ch", "col")

    def swap(value):
        return lax.ppermute(value, "core", [(0, 1), (1, 0)])

    def across(value, mask):
        return lax.ppermute(value, "ch", [(i, i ^ mask) for i in range(chip_rows)])

    def exchange(value):
        return lax.all_to_all(value, every, 0, 0, tiled=True)

    at = jnp.concatenate([row, col.reshape(1)])

    lists = neighbours.reshape(-1, MXU)
    lists = jnp.stack([lists] + [across(lists, mask) for mask in range(1, chip_rows)])
    own = lax.all_to_all(features, every, 1, 0, tiled=True)
    turned = count_tile(at, lists, nodes, cols, True)
    tile_own = count_tile(at, lists, nodes, cols, False)
    tile_other = count_tile(at, swap(lists), nodes, cols, False)

    own_lists = lax.dynamic_slice_in_dim(neighbours, col * nodes, nodes, 0)
    inverse = 1.0 / (jnp.sum(own_lists >= 0, axis=1).astype(F32) + 1.0)
    inverse = inverse.reshape(1, nodes)
    valid = valid_mask.astype(F32).reshape(nodes, 1)

    def to_plane(parts):
        return [parts[0]] + [across(parts[mask], mask) for mask in range(1, chip_rows)]

    def both_cores(parts):
        return [part for one in parts for part in (one, swap(one))]

    def along(value, mask):
        return lax.ppermute(value, "col", [(i, i ^ mask) for i in range(cols)])

    def exchange_beside(value, *others):
        return lax.optimization_barrier((exchange(value), *others))

    own, turned = lax.optimization_barrier((own, turned))
    agg_one = exchange(apply_adjacency([turned], own, swap(own), True))
    agg_one, tile_own = lax.optimization_barrier((agg_one, tile_own))
    hidden, slope_one, stats_one, *pieces_one = first_layer(
        at, agg_one, weight_one, bias_one.reshape(1, -1), valid, features, chip_rows
    )
    own, tile_other = exchange_beside(hidden, tile_other)
    agg_two = apply_adjacency([turned], own, swap(own), True)
    agg_two, *pieces_one = exchange_beside(agg_two, *to_plane(pieces_one))
    act, grad_pre_two, sums_two, grad_agg_two, *pieces_two = second_layer(
        at, agg_two, weight_two, bias_two.reshape(1, -1), valid, cotangent, inverse, stats_one, chip_rows
    )
    cut = nodes // 2

    def backward_one(grads, grad_pre, *others):
        own, by_x, by_y, core_other, *others = exchange_beside(
            grads, across(grad_pre, 1), across(grad_pre, 2), swap(grad_pre), *others
        )
        diagonal = across(by_x, 2)
        sums = apply_adjacency([tile_own, tile_other], own, swap(own), False)
        sums, by_x, by_y = lax.optimization_barrier((sums, by_x, by_y))
        return sums, [grad_pre, core_other, *both_cores([by_x, by_y, diagonal])], others

    def backward_two(grads, grad_pre, *others):
        own, by_x, by_y, core_other, *others = exchange_beside(
            grads, across(grad_pre, 1), across(grad_pre, 2), swap(grad_pre), *others
        )
        diagonal = [across(by_x[:cut], 2), across(by_y[cut:], 1)]
        sums = apply_adjacency([tile_own, tile_other], own, swap(own), False)
        sums, by_x, by_y, *diagonal = lax.optimization_barrier((sums, by_x, by_y, *diagonal))
        return sums, [grad_pre, core_other, *both_cores([by_x, by_y]), *both_halves(diagonal)], others

    def both_halves(diagonal):
        return diagonal + [swap(part) for part in diagonal]

    sums, plane_two, _ = backward_two(sums_two, grad_pre_two)
    sums, *pieces_two = lax.optimization_barrier((sums, *pieces_two))
    upstream, *pieces_two = exchange_beside(sums, *to_plane(pieces_two))
    grad_pre_one, sums_one, grad_agg_one = first_layer_back(slope_one, weight_one, inverse, upstream, grad_agg_two)
    kept_two, sent_two = weight_product(at, both_cores(pieces_two), plane_two, ((0, 2), (1, 3)))
    sums, plane_one, (kept_two, sent_two) = backward_one(sums_one, grad_pre_one, kept_two, sent_two)
    grad_start = input_gradient(exchange(sums), grad_agg_one, inverse)
    pair_two = along(sent_two, 1)
    last_two, plane_one[0] = lax.optimization_barrier((pair_sum(kept_two, pair_two), plane_one[0]))
    last_two = along(last_two, 2)
    parts_one = weight_product(at, both_cores(pieces_one), plane_one, tuple((mask,) for mask in range(cols)))
    parts_one = [part if mask == 0 else along(part, mask) for mask, part in enumerate(parts_one)]
    last_two, grad_start = lax.optimization_barrier((last_two, grad_start))
    weight_grad_two, bias_grad_two, rms_stats = sum_pieces([kept_two, pair_two, last_two])
    *parts_one, weight_grad_two = lax.optimization_barrier((*parts_one, weight_grad_two))
    weight_grad_one, bias_grad_one, _ = sum_pieces(parts_one)
    bias_grad_one, bias_grad_two = bias_grad_one.reshape(-1), bias_grad_two.reshape(-1)
    return (act, grad_start, weight_grad_one, bias_grad_one, weight_grad_two, bias_grad_two, rms_stats)


def solution(mesh):
    rows, cols = mesh.devices.shape
    axes = ("ch", "core", "col")
    wide = Mesh(mesh.devices.reshape(rows // 2, 2, cols), axes)

    def program(features, *rest):
        nodes, full = features.shape
        slots = rest[5].shape[1]
        fits = (
            (rows, cols) == (8, 4)
            and nodes == rows * cols * LANES
            and full == rows * cols * 64
            and slots * nodes == MXU * MXU
            and slots == 16
        )
        split, over = (axes, wide) if fits else (("row", "col"), mesh)
        lists = ("ch", "core") if fits else "row"
        spread = P(split, None)
        return jax.shard_map(
            transposed if fits else general,
            mesh=over,
            in_specs=(spread, P(), P(), P(), P(), spread, P(lists, None), P(split)),
            out_specs=(spread, spread, spread, P(split), spread, P(split), P()),
            check_vma=False,
        )(features, *rest)

    return program
```

```python
import functools

import jax
import jax.numpy as jnp
from jax import lax
from jax.experimental import pallas as pl
from jax.experimental.pallas import tpu as pltpu
from jax.sharding import Mesh
from jax.sharding import PartitionSpec as P

BF16, F32 = jnp.bfloat16, jnp.float32
LANES = 128
MXU = 256
MIB = 1 << 20
NT = (((1,), (1,)), ((), ()))
GELU_C, GELU_A = 0.7978845608, 0.044715


def gelu_value(value):
    return jax.nn.gelu(value, approximate=True)


def source_parts(lists, per_dev, col_devs):
    live = lists >= 0
    safe = jnp.maximum(lists, 0)
    block = safe // per_dev
    return (live, block // col_devs, block % col_devs, safe % per_dev)


def block_tile(lists, usable, local_index, span):
    columns = jnp.arange(span, dtype=jnp.int32)[None, :]
    marked = jnp.where(usable, local_index, -1)
    total = jnp.zeros((lists.shape[0], span), jnp.float32)
    for slot in range(lists.shape[1]):
        total = total + (marked[:, slot : slot + 1] == columns).astype(jnp.float32)
    return total.astype(jnp.bfloat16)


def reduce_weights(grad_weight, grad_bias):
    return (
        lax.psum_scatter(grad_weight, ("row", "col"), scatter_dimension=0, tiled=True),
        lax.psum_scatter(grad_bias, ("row", "col"), scatter_dimension=0, tiled=True),
    )


def general(features, weight_one, bias_one, weight_two, bias_two, cotangent, neighbours, valid_mask):
    per_dev, width = features.shape
    row_devs = lax.axis_size("row")
    col_devs = lax.axis_size("col")
    col_pos = lax.axis_index("col")
    own_lists = lax.dynamic_slice_in_dim(neighbours, col_pos * per_dev, per_dev, 0)
    inverse = 1.0 / (jnp.sum(own_lists >= 0, axis=1).astype(jnp.float32) + 1.0)
    scaling = inverse[:, None]
    validity = valid_mask.astype(jnp.float32)[:, None]
    live, src_row, src_col, offset = source_parts(neighbours, per_dev, col_devs)
    front_tile = block_tile(
        neighbours, live & (src_col == col_pos), src_row * per_dev + offset, row_devs * per_dev
    )

    def forward_layer(inputs, weight, bias):
        gathered = lax.all_gather(inputs, "row", axis=0, tiled=True)
        partial_value = jnp.dot(front_tile, gathered, preferred_element_type=jnp.float32)
        summed = lax.psum_scatter(partial_value, "col", scatter_dimension=0, tiled=True)
        aggregate = ((summed + 2.0 * inputs.astype(jnp.float32)) * scaling).astype(jnp.bfloat16)
        preact = jnp.dot(aggregate, weight, preferred_element_type=jnp.float32) + bias
        return (aggregate, preact, validity * gelu_value(preact))

    agg_one, pre_one, out_one = forward_layer(features, weight_one, bias_one)
    hidden = out_one.astype(jnp.bfloat16)
    agg_two, pre_two, out_two = forward_layer(hidden, weight_two, bias_two)

    def squares(value):
        return jnp.sum(validity * jnp.square(value.astype(jnp.float32)))

    local_squares = jnp.stack(
        [
            squares(features),
            squares(agg_one),
            squares(out_one),
            squares(hidden),
            squares(agg_two),
            squares(out_two),
        ]
    ).reshape(2, 3)
    total_squares, total_valid = lax.psum((local_squares, jnp.sum(validity)), ("row", "col"))
    rms_stats = jnp.sqrt(total_squares / (total_valid * width) + 1e-06)

    def backward_layer(upstream, aggregate, preact, weight):
        grad_act = validity * upstream
        grad_pre = jax.vjp(gelu_value, preact)[1](grad_act)[0].astype(jnp.bfloat16)
        grad_weight = lax.dot_general(
            aggregate, grad_pre, (((0,), (0,)), ((), ())), preferred_element_type=jnp.float32
        )
        grad_bias = jnp.sum(grad_pre.astype(jnp.float32), axis=0)
        grad_low = lax.dot_general(
            grad_pre, weight, (((1,), (1,)), ((), ())), preferred_element_type=jnp.float32
        ).astype(jnp.bfloat16)
        grad_agg = lax.optimization_barrier(grad_low).astype(jnp.float32)
        grad_sum = (grad_agg * scaling).astype(jnp.bfloat16)
        grad_all = lax.all_gather(grad_sum, "col", axis=0, tiled=True)
        from_lists = lax.psum_scatter(
            lax.dot_general(
                front_tile, grad_all, (((0,), (0,)), ((), ())), preferred_element_type=jnp.float32
            ),
            "row",
            scatter_dimension=0,
            tiled=True,
        )
        return (from_lists + 2.0 * grad_agg * scaling, grad_weight, grad_bias)

    grad_hidden, weight_grad_two, bias_grad_two = backward_layer(
        cotangent.astype(jnp.float32), agg_two, pre_two, weight_two
    )
    weight_grad_two, bias_grad_two = reduce_weights(weight_grad_two, bias_grad_two)
    grad_start, weight_grad_one, bias_grad_one = backward_layer(
        grad_hidden, agg_one, pre_one, weight_one
    )
    weight_grad_one, bias_grad_one = reduce_weights(weight_grad_one, bias_grad_one)
    return (
        out_two.astype(jnp.bfloat16),
        grad_start.astype(jnp.bfloat16),
        weight_grad_one,
        bias_grad_one,
        weight_grad_two,
        bias_grad_two,
        rms_stats,
    )


IN_VMEM = pl.BlockSpec(memory_space=pltpu.VMEM)
IN_SMEM = pl.BlockSpec(memory_space=pltpu.SMEM)
IN_ANY = pl.BlockSpec(memory_space=pl.ANY)
COUNT = jnp.float8_e4m3fn
PARAMS = pltpu.CompilerParams(vmem_limit_bytes=48 * MIB)


def cost(flops, read, transcendentals=0):
    return pl.CostEstimate(flops=flops, bytes_accessed=read, transcendentals=transcendentals)


def lanes(at, size=LANES):
    return slice(at * size, (at + 1) * size)


def fetch(source, target, semaphore):
    copy = pltpu.make_async_copy(source, target, semaphore)
    copy.start()
    return copy


def stream(source, blocks, target, semaphores):
    copies = [fetch(source.at[block], target.at[block], semaphores.at[i]) for i, block in enumerate(blocks)]

    def arrivals():
        for block, copy in zip(blocks, copies, strict=True):
            copy.wait()
            yield target[block]

    return arrivals()


def buffer(shape, blocks, dtype=BF16):
    return [pltpu.VMEM(shape, dtype), pltpu.SemaphoreType.DMA((blocks,))]


def like(value):
    return [pltpu.VMEM(value.shape, value.dtype), pltpu.SemaphoreType.DMA]


class Results:
    def __init__(self, semaphores):
        self.semaphores, self.copies = semaphores, []

    def send(self, source, target):
        self.copies.append(fetch(source, target, self.semaphores.at[len(self.copies)]))

    def wait(self):
        for copy in self.copies:
            copy.wait()


def column_blocks(size, step):
    return [(slice(None), slice(at, at + step)) for at in range(0, size, step)]


def row_blocks(size, step):
    return [(slice(at, at + step), slice(None)) for at in range(0, size, step)]


def tile_kernel(turn, nodes, cols, place_ref, lists_ref, tile_ref):
    masks, lines, width = lists_ref.shape
    groups = 8
    rows = LANES // groups
    chip_row, core = place_ref[0] // 2, place_ref[0] % 2
    step = pl.program_id(0)
    per_chip = lines // groups
    mask = chip_row ^ (step // per_chip)
    lists = lists_ref[mask, pl.ds(pl.multiple_of(step % per_chip * groups, groups), groups), :]
    node_bits, col_bits = nodes.bit_length() - 1, cols.bit_length() - 1
    owner_row = lists >> (node_bits + col_bits)
    within = lists & (nodes * cols - 1)
    place = ((owner_row >> 1) << (node_bits + col_bits)) + within
    live = lists >= 0
    if turn:
        half = masks * cols * nodes
        place = jnp.where((owner_row & 1) == core, place, place + half)
    else:
        live &= (owner_row & 1) == core
    line = lax.broadcasted_iota(jnp.int32, lists.shape, 1) // rows
    highs = jnp.where(live, (place // MXU) * rows + line, -1)
    lows = place % MXU
    blocks = (tile_ref.shape[0] if turn else tile_ref.shape[1]) // MXU
    high_place = lax.broadcasted_iota(jnp.int32, (blocks * rows, width), 0)
    low_place = lax.broadcasted_iota(jnp.int32, (MXU, width), 0)
    pieces = []
    for group in range(groups):
        high = (high_place == highs[group : group + 1, :]).astype(F32).astype(BF16)
        low = (low_place == lows[group : group + 1, :]).astype(F32).astype(BF16)
        counts = lax.dot_general(high, low, NT, preferred_element_type=F32)
        pieces.append(counts.astype(BF16))
    for block in range(blocks):
        column = jnp.concatenate([piece[block * rows : (block + 1) * rows] for piece in pieces], axis=0)
        if turn:
            for side in range(2):
                turned = column[:, lanes(side)].T
                tile_ref[lanes(2 * block + side), :] = turned.astype(COUNT)
        else:
            tile_ref[:, lanes(block, MXU)] = column.astype(COUNT)


def count_tile(at, lists, nodes, cols, turn):
    masks, lines, width = lists.shape
    rows = masks * lines * 16
    half = masks * cols * nodes
    shape = (2 * half, rows) if turn else (rows, half)
    block = (2 * half, LANES) if turn else (LANES, half)
    return pl.pallas_call(
        functools.partial(tile_kernel, turn, nodes, cols),
        grid=(rows // LANES,),
        in_specs=[IN_SMEM, pl.BlockSpec(lists.shape, lambda i: (0, 0, 0))],
        out_specs=pl.BlockSpec(block, (lambda i: (0, i)) if turn else (lambda i: (i, 0))),
        out_shape=jax.ShapeDtypeStruct(shape, COUNT),
        compiler_params=PARAMS,
        cost_estimate=cost(4 * rows * shape[0 if turn else 1] * 2 * MXU, rows * half),
    )(at, lists)


def adjacency_kernel(forward, tiles, own_ref, other_ref, *refs):
    tile_refs, refs = refs[:tiles], refs[-10 - tiles :]
    out_ref, left_ref, total_ref, own, own_sem, other, other_sem = refs[:7]
    buffers, (semaphores, out, out_sems) = refs[7 : 7 + tiles], refs[7 + tiles :]
    chips, width = own_ref.shape[0], LANES
    half = chips * width
    copies = [fetch(own_ref, own, own_sem), fetch(other_ref, other, other_sem)]
    chunks, arrivals = [], []
    for ref, target in zip(tile_refs, buffers, strict=True):
        for at in range(0, ref.shape[0], half):
            here = slice(at, at + half)
            arrivals.append(fetch(ref.at[here], target.at[here], semaphores.at[len(chunks)]))
            chunks.append(target.at[here])
    for copy in copies:
        copy.wait()
    for at in range(chips):
        left_ref[:width, lanes(at)] = own[at].T if forward else own[at]
        left_ref[:width, lanes(chips + at)] = other[at].T if forward else other[at]
    if forward:
        left_ref[width:, :] = jnp.ones((left_ref.shape[0] - width, left_ref.shape[1]), BF16)
    for block, (copy, counts) in enumerate(zip(arrivals, chunks, strict=True)):
        copy.wait()
        part = jnp.dot(left_ref[:, lanes(block, half)], counts[...].astype(BF16), preferred_element_type=F32)
        if block == 0:
            total_ref[...] = part
        else:
            total_ref[...] += part
    results = Results(out_sems)
    group = chips // out_sems.shape[0]
    for at in range(chips):
        here = lanes(at)
        if forward:
            inverse = 1.0 / (total_ref[width : width + 1, here] + 1.0)
            value = (total_ref[:width, here] + 2.0 * left_ref[:width, here].astype(F32)) * inverse
            out[at] = value.astype(BF16).T
        else:
            out[at] = total_ref[:, here].astype(BF16)
        if (at + 1) % group == 0:
            done = slice(at + 1 - group, at + 1)
            results.send(out.at[done], out_ref.at[done])
    results.wait()


def apply_adjacency(tiles, own, other, forward, *after):
    sources, half = sum(tile.shape[0] for tile in tiles), tiles[0].shape[1]
    rows = LANES + (16 if forward else 0)
    scratch = [pltpu.VMEM((rows, sources), BF16), pltpu.VMEM((rows, half), F32)] + like(own) + like(other)
    scratch += [pltpu.VMEM(tile.shape, COUNT) for tile in tiles] + [pltpu.SemaphoreType.DMA((sources // half,))]
    return pl.pallas_call(
        functools.partial(adjacency_kernel, forward, len(tiles)),
        in_specs=[IN_ANY] * (2 + len(tiles) + len(after)),
        out_specs=IN_ANY,
        out_shape=jax.ShapeDtypeStruct(own.shape, BF16),
        scratch_shapes=scratch + buffer(own.shape, 4),
        compiler_params=PARAMS,
        cost_estimate=cost(2 * half * sources * LANES, half * sources),
    )(own, other, *tiles, *after)


def gelu_parts(pre, valid):
    square = pre * pre
    bend = jnp.tanh(GELU_C * (pre + GELU_A * (square * pre)))
    inner = GELU_C * (1.0 + 3.0 * GELU_A * square)
    slope = 0.5 * (1.0 + bend) + 0.5 * pre * (1.0 - bend * bend) * inner
    return valid * (0.5 * pre * (1.0 + bend)), valid * slope


def lane_squares(value, valid):
    value = value.astype(F32)
    value = jnp.sum(valid * (value * value), axis=0, keepdims=True)
    return sum(value[:, lanes(i)] for i in range(value.shape[1] // LANES))


def send_pieces(at_ref, agg_blocks, pieces, piece_refs, results):
    chip_row = at_ref[0] // 2
    blocks = agg_blocks.shape[0] // len(piece_refs)
    for mask, ref in enumerate(piece_refs):
        for part in range(blocks):
            pieces[mask, :, lanes(part)] = agg_blocks[(chip_row ^ mask) * blocks + part]
        results.send(pieces.at[mask], ref)


def first_kernel(at_ref, agg_ref, weight_ref, bias_ref, valid_ref, input_ref, *refs):
    out_ref, slope_ref, stat_ref = refs[-17:-14]
    piece_refs = refs[-14:-10]
    agg_blocks, agg_sem, inputs, input_sem, weight_buffer, semaphores = refs[-10:-4]
    out, slopes, pieces, out_sems = refs[-4:]
    chips, nodes, width = agg_ref.shape
    full = weight_ref.shape[1]
    step = full // semaphores.shape[0]
    copies = [fetch(agg_ref, agg_blocks, agg_sem)]
    weights = stream(weight_ref, column_blocks(full, step), weight_buffer, semaphores)
    copies.append(fetch(input_ref, inputs, input_sem))
    results = Results(out_sems)
    valid = valid_ref[...]
    copies[0].wait()
    agg = jnp.concatenate([agg_blocks[i] for i in range(chips)], axis=1)
    send_pieces(at_ref, agg_blocks, pieces, piece_refs, results)
    none = jnp.zeros((1, LANES), F32)
    of_agg, of_input, of_out, of_low = lane_squares(agg, valid), none, none, none
    for block, weight in enumerate(weights):
        here = lanes(block, step)
        pre = jnp.dot(agg, weight, preferred_element_type=F32) + bias_ref[:, here]
        value, slopes[:, here] = gelu_parts(pre, valid)
        low = value.astype(BF16)
        of_out += lane_squares(value, valid)
        of_low += lane_squares(low, valid)
        if block == 0:
            copies[1].wait()
        of_input += lane_squares(inputs[:, here], valid)
        blocks = lanes(block, step // LANES)
        for part in range(step // LANES):
            out[blocks.start + part] = low[:, lanes(part)]
        results.send(out.at[blocks], out_ref.at[blocks])
        results.send(slopes.at[:, here], slope_ref.at[:, here])
    count = jnp.sum(jnp.broadcast_to(valid, (nodes, LANES)), axis=0, keepdims=True) * (1.0 / LANES)
    stat_ref[...] = jnp.concatenate([of_input, of_agg, of_out, of_low, count, none, none, none], axis=0)
    results.wait()


def piece_shapes(agg, chip_rows):
    chips, nodes, width = agg.shape
    return [jax.ShapeDtypeStruct((nodes, chips * width // chip_rows), BF16)] * chip_rows


def first_layer(at, agg, weight, bias, valid, inputs, chip_rows, *after):
    chips, nodes, width = agg.shape
    full = weight.shape[1]
    pieces = piece_shapes(agg, chip_rows)
    steps = 2
    return pl.pallas_call(
        first_kernel,
        in_specs=[IN_SMEM, IN_ANY, IN_ANY, IN_VMEM, IN_VMEM, IN_ANY] + [IN_ANY] * len(after),
        out_specs=[IN_ANY, IN_ANY, IN_VMEM] + [IN_ANY] * chip_rows,
        out_shape=[
            jax.ShapeDtypeStruct(agg.shape, BF16),
            jax.ShapeDtypeStruct((nodes, full), F32),
            jax.ShapeDtypeStruct((8, LANES), F32),
        ]
        + pieces,
        scratch_shapes=like(agg)
        + like(inputs)
        + buffer(weight.shape, steps)
        + [
            pltpu.VMEM(agg.shape, BF16),
            pltpu.VMEM((nodes, full), F32),
            pltpu.VMEM((chip_rows,) + pieces[0].shape, BF16),
            pltpu.SemaphoreType.DMA((chip_rows + 2 * steps,)),
        ],
        compiler_params=PARAMS,
        cost_estimate=cost(2 * nodes * full * full, 2 * full * full, nodes * full),
    )(at, agg, weight, bias, valid, inputs, *after)


def gradient_blocks(weight, blocks, turned, inverse, outs, refs, results):
    low = jnp.dot(weight, turned[...], preferred_element_type=F32).astype(BF16)
    sums = (low.astype(F32) * inverse).astype(BF16)
    for value, out, ref in zip((sums, low), outs, refs, strict=True):
        for part in range(weight.shape[0] // LANES):
            out[blocks.start + part] = value[lanes(part)]
        results.send(out.at[blocks], ref.at[blocks])


def second_kernel(
    at_ref, agg_ref, weight_ref, bias_ref, valid_ref, cotangent_ref, inverse_ref, stat_ref, *refs
):
    act_ref, pre_ref, sums_ref, grad_agg_ref = refs[-21:-17]
    piece_refs = refs[-17:-13]
    agg_blocks, agg_sem, cotangent, cotangent_sem, weight_buffer, semaphores = refs[-13:-7]
    act, pres, turned, sums, grad_agg, pieces, out_sems = refs[-7:]
    chips, nodes, width = agg_ref.shape
    full = weight_ref.shape[1]
    step = full // semaphores.shape[0]
    copies = [fetch(agg_ref, agg_blocks, agg_sem)]
    weights = stream(weight_ref, column_blocks(full, step), weight_buffer, semaphores)
    copies.append(fetch(cotangent_ref, cotangent, cotangent_sem))
    results = Results(out_sems)
    valid, inverse = valid_ref[...], inverse_ref[...]
    copies[0].wait()
    agg = jnp.concatenate([agg_blocks[i] for i in range(chips)], axis=1)
    send_pieces(at_ref, agg_blocks, pieces, piece_refs, results)
    of_agg, of_out = lane_squares(agg, valid), jnp.zeros((1, LANES), F32)
    for block, weight in enumerate(weights):
        here = lanes(block, step)
        pre = jnp.dot(agg, weight, preferred_element_type=F32) + bias_ref[:, here]
        value, slope = gelu_parts(pre, valid)
        of_out += lane_squares(value, valid)
        act[:, here] = value.astype(BF16)
        results.send(act.at[:, here], act_ref.at[:, here])
        if block == 0:
            copies[1].wait()
        grad_pre = (cotangent[:, here].astype(F32) * slope).astype(BF16)
        pres[:, here] = grad_pre
        for part in range(step // LANES):
            turned[block * step + part * LANES : block * step + (part + 1) * LANES, :] = grad_pre[:, lanes(part)].T
    stat = stat_ref[...]
    rows = [stat[:4], of_agg, of_out, stat[4:5], jnp.zeros((1, LANES), F32)]
    total = jnp.sum(jnp.concatenate(rows, axis=0), axis=1, keepdims=True)
    high = total.astype(BF16).astype(F32)
    both = jnp.concatenate([high, total - high], axis=0)
    pres[:16, full:] = jnp.broadcast_to(both, (16, LANES)).astype(BF16)
    pres[16:, full:] = jnp.zeros((nodes - 16, LANES), BF16)
    results.send(pres, pre_ref)
    step = full // 4
    for block in range(4):
        gradient_blocks(
            weight_buffer[lanes(block, step), :], lanes(block, step // LANES), turned, inverse,
            (sums, grad_agg), (sums_ref, grad_agg_ref), results,
        )
    results.wait()


def second_layer(at, agg, weight, bias, valid, cotangent, inverse, stats, chip_rows, *after):
    chips, nodes, width = agg.shape
    full = weight.shape[1]
    blocks = jax.ShapeDtypeStruct((chips, width, nodes), BF16)
    pieces = piece_shapes(agg, chip_rows)
    steps = 2
    return pl.pallas_call(
        second_kernel,
        in_specs=[IN_SMEM, IN_ANY, IN_ANY, IN_VMEM, IN_VMEM, IN_ANY, IN_VMEM, IN_VMEM] + [IN_ANY] * len(after),
        out_specs=[IN_ANY] * (4 + chip_rows),
        out_shape=[
            jax.ShapeDtypeStruct((nodes, full), BF16),
            jax.ShapeDtypeStruct((nodes, full + LANES), BF16),
            blocks,
            blocks,
        ]
        + pieces,
        scratch_shapes=like(agg)
        + like(cotangent)
        + buffer(weight.shape, steps)
        + [
            pltpu.VMEM((nodes, full), BF16),
            pltpu.VMEM((nodes, full + LANES), BF16),
            pltpu.VMEM((full, nodes), BF16),
            pltpu.VMEM(blocks.shape, BF16),
            pltpu.VMEM(blocks.shape, BF16),
            pltpu.VMEM((chip_rows,) + pieces[0].shape, BF16),
            pltpu.SemaphoreType.DMA((chip_rows + steps + 1 + 8,)),
        ],
        compiler_params=PARAMS,
        cost_estimate=cost(4 * nodes * full * full, 2 * full * full, nodes * full),
    )(at, agg, weight, bias, valid, cotangent, inverse, stats, *after)


def back_kernel(slope_ref, weight_ref, inverse_ref, up_ref, extra_ref, *refs):
    pre_ref, sums_ref, agg_ref, slope, slope_sem, up, up_sem, extra, extra_sem = refs[-16:-7]
    weight_buffer, semaphores, pres, turned, sums, grad_agg, out_sems = refs[-7:]
    nodes, full = slope_ref.shape
    step = full // semaphores.shape[0]
    copies = [fetch(up_ref, up, up_sem), fetch(extra_ref, extra, extra_sem), fetch(slope_ref, slope, slope_sem)]
    weights = stream(weight_ref, row_blocks(full, step), weight_buffer, semaphores)
    results = Results(out_sems)
    inverse = inverse_ref[...]
    for copy in copies:
        copy.wait()
    for at in range(up_ref.shape[0]):
        value = up[at].astype(F32) + 2.0 * extra[at].astype(F32) * inverse
        grad_pre = (value.T * slope[:, lanes(at)]).astype(BF16)
        pres[:, lanes(at)] = grad_pre
        turned[lanes(at), :] = grad_pre.T
    pres[:, full:] = jnp.zeros((nodes, LANES), BF16)
    results.send(pres, pre_ref)
    for block, weight in enumerate(weights):
        gradient_blocks(
            weight, lanes(block, step // LANES), turned, inverse, (sums, grad_agg), (sums_ref, agg_ref), results
        )
    results.wait()


def first_layer_back(slope, weight, inverse, upstream, extra, *after):
    nodes, full = slope.shape
    blocks = jax.ShapeDtypeStruct(upstream.shape, BF16)
    steps = 1
    return pl.pallas_call(
        back_kernel,
        in_specs=[IN_ANY, IN_ANY, IN_VMEM, IN_ANY, IN_ANY] + [IN_ANY] * len(after),
        out_specs=[IN_ANY] * 3,
        out_shape=[jax.ShapeDtypeStruct((nodes, full + LANES), BF16), blocks, blocks],
        scratch_shapes=like(slope)
        + like(upstream)
        + like(extra)
        + buffer(weight.shape, steps)
        + [
            pltpu.VMEM((nodes, full + LANES), BF16),
            pltpu.VMEM((full, nodes), BF16),
            pltpu.VMEM(blocks.shape, BF16),
            pltpu.VMEM(blocks.shape, BF16),
            pltpu.SemaphoreType.DMA((1 + 2 * steps,)),
        ],
        compiler_params=PARAMS,
        cost_estimate=cost(2 * nodes * full * full, 2 * full * full),
    )(slope, weight, inverse, upstream, extra, *after)


def left_factor(at_ref, lefts, left_parts, left_sem, left_ref):
    nodes = lefts[0].shape[0]
    width = left_parts.shape[2]
    mine = pl.ds(pl.multiple_of(at_ref[0] % 2 * width, width), width)
    copies = [fetch(ref.at[:, mine], left_parts.at[i], left_sem.at[i]) for i, ref in enumerate(lefts)]

    def finish():
        for i, copy in enumerate(copies):
            copy.wait()
            left_ref[:width, lanes(i, nodes)] = left_parts[i].T
        left_ref[width:, :] = jnp.ones((left_ref.shape[0] - width, left_ref.shape[1]), BF16)

    return finish


def products(at_ref, left_ref, right, copies, width, use):
    bias = jnp.zeros((8, width), F32)
    step = right.shape[1] // len(copies)
    for block, group in enumerate(copies):
        for copy in group:
            copy.wait()
        here = lanes(block, step)
        total = jnp.dot(left_ref[...], right[:, here], preferred_element_type=F32)
        use(here, total)
        for part in range(step // width):
            one = block * (step // width) + part
            bias += jnp.where(at_ref[0] == one, total[width : width + 8, lanes(part, width)], 0.0)
    return bias


def small_sums(bias, stats, rows):
    high, stats_high = bias.astype(BF16).astype(F32), stats.astype(BF16).astype(F32)
    line = lax.broadcasted_iota(jnp.int32, (8, LANES), 0)
    first = jnp.where(line == 0, high, jnp.where(line == 1, bias - high, 0.0))
    rest = jnp.zeros((rows - 24, LANES), F32)
    return jnp.concatenate([first, stats_high, stats - stats_high, rest], axis=0).astype(BF16)


def read_small(extra):
    return extra[0:1] + extra[1:2], extra[8:16] + extra[16:24]


def weight_kernel(masks, at_ref, *refs):
    lefts, rights, outs = refs[:8], refs[8 : -7 - len(masks)], refs[-7 - len(masks) : -7]
    left_parts, left_sem, right, right_sems, stat_parts, stat_sems, left_ref = refs[-7:]
    col = at_ref[1]
    full = outs[0].shape[1] - LANES
    piece_rows = outs[0].shape[0] // len(masks[0])
    pieces = sum(len(group) for group in masks)
    nodes, width = left_parts.shape[1:]
    finish = left_factor(at_ref, lefts, left_parts, left_sem, left_ref)
    steps = right_sems.shape[0]
    starts = [sum(ref.shape[0] for ref in rights[:i]) for i in range(len(rights))]
    copies = [
        [
            fetch(
                ref.at[:, lanes(block, full // steps)],
                right.at[slice(start, start + ref.shape[0]), lanes(block, full // steps)],
                right_sems.at[block, i],
            )
            for i, (ref, start) in enumerate(zip(rights, starts, strict=True))
        ]
        for block in range(steps)
    ]
    firsts = [ref for ref, start in zip(rights, starts, strict=True) if start % nodes == 0]
    stat_copies = [
        fetch(ref.at[:16, slice(full, full + LANES)], stat_parts.at[i], stat_sems.at[i])
        for i, ref in enumerate(firsts)
    ]
    finish()

    def use(here, total):
        for group, ref in zip(masks, outs, strict=True):
            for at, mask in enumerate(group):
                value = total[:piece_rows]
                for piece in range(1, pieces):
                    value = jnp.where(col ^ mask == piece, total[lanes(piece, piece_rows)], value)
                ref[lanes(at, piece_rows), here] = value.astype(BF16)

    bias = products(at_ref, left_ref, right, copies, width, use)
    stats = jnp.zeros((8, LANES), F32)
    for i, copy in enumerate(stat_copies):
        copy.wait()
        both = stat_parts[i].astype(F32)
        stats += both[:8] + both[8:]
    for group, ref in zip(masks, outs, strict=True):
        for at, mask in enumerate(group):
            piece = col ^ mask
            one = jnp.where(piece >= 2, bias[:, LANES:], bias[:, :LANES])
            one = jnp.where(piece % 2 == 1, pltpu.roll(one, LANES // 2, 1), one)
            ref[lanes(at, piece_rows), full:] = small_sums(one, stats, piece_rows)


def weight_product(at, lefts, rights, masks):
    nodes, full = lefts[0].shape[0], rights[0].shape[1]
    full -= LANES
    width = lefts[0].shape[1] // 2
    rows = width // sum(len(group) for group in masks)
    return pl.pallas_call(
        functools.partial(weight_kernel, masks),
        in_specs=[IN_SMEM] + [IN_ANY] * (8 + len(rights)),
        out_specs=[IN_VMEM] * len(masks),
        out_shape=[jax.ShapeDtypeStruct((rows * len(group), full + LANES), BF16) for group in masks],
        scratch_shapes=[
            pltpu.VMEM((8, nodes, width), BF16),
            pltpu.SemaphoreType.DMA((8,)),
            pltpu.VMEM((8 * nodes, full), BF16),
            pltpu.SemaphoreType.DMA((2, len(rights))),
            pltpu.VMEM((8, 16, LANES), BF16),
            pltpu.SemaphoreType.DMA((8,)),
            pltpu.VMEM((width + 16, 8 * nodes), BF16),
        ],
        compiler_params=PARAMS,
        cost_estimate=cost(2 * 8 * nodes * full * width, 4 * 8 * nodes * full),
    )(at, *lefts, *rights)


def pair_kernel(one_ref, two_ref, out_ref):
    rows, full = out_ref.shape
    full -= LANES
    step = 512
    for at in range(0, full, step):
        here = slice(at, at + step)
        out_ref[:, here] = (one_ref[rows:, here].astype(F32) + two_ref[rows:, here].astype(F32)).astype(BF16)
    bias, stats = read_small(one_ref[rows:, full:].astype(F32) + two_ref[rows:, full:].astype(F32))
    out_ref[:, full:] = small_sums(bias, stats, rows)


def pair_sum(one, two):
    return pl.pallas_call(
        pair_kernel,
        in_specs=[IN_VMEM] * 2,
        out_specs=IN_VMEM,
        out_shape=jax.ShapeDtypeStruct((one.shape[0] // 2, one.shape[1]), BF16),
        compiler_params=PARAMS,
    )(one, two)


def sum_kernel(*refs):
    parts, (out_ref, bias_ref, rms_ref) = refs[:-3], refs[-3:]
    rows, full = out_ref.shape
    count = bias_ref.shape[1]

    def total(here):
        return sum([part[:rows, here].astype(F32) for part in parts[1:]], parts[0][:rows, here].astype(F32))

    step = 512
    for at in range(0, full, step):
        out_ref[:, at : at + step] = total(slice(at, at + step))
    bias, stats = read_small(total(slice(full, full + LANES)))
    bias_ref[...] = bias[:, :count]
    rms = jnp.sqrt(stats / jnp.maximum(stats[6:7] * full, 1.0) + 1e-06)
    row = lax.broadcasted_iota(jnp.int32, rms_ref.shape, 0)
    place = 3 * row + lax.broadcasted_iota(jnp.int32, rms_ref.shape, 1)
    value = jnp.zeros(rms_ref.shape, F32)
    for at in range(6):
        value = jnp.where(place == at, rms[at : at + 1, :3], value)
    rms_ref[...] = value


def sum_pieces(parts):
    rows, full = parts[-1].shape
    full -= LANES
    return pl.pallas_call(
        sum_kernel,
        in_specs=[IN_VMEM] * len(parts),
        out_specs=[IN_VMEM] * 3,
        out_shape=[
            jax.ShapeDtypeStruct((rows, full), F32),
            jax.ShapeDtypeStruct((1, rows), F32),
            jax.ShapeDtypeStruct((2, 3), F32),
        ],
        compiler_params=PARAMS,
    )(*parts)


def final_kernel(up_ref, agg_ref, inverse_ref, out_ref):
    inverse = inverse_ref[...]
    for at in range(up_ref.shape[0]):
        value = up_ref[at].astype(F32) + 2.0 * agg_ref[at].astype(F32) * inverse
        out_ref[:, lanes(at)] = value.T.astype(BF16)


def input_gradient(upstream, grad_agg, inverse):
    chips, width, nodes = upstream.shape
    return pl.pallas_call(
        final_kernel,
        in_specs=[IN_VMEM] * 3,
        out_specs=IN_VMEM,
        out_shape=jax.ShapeDtypeStruct((nodes, chips * width), BF16),
        compiler_params=PARAMS,
    )(upstream, grad_agg, inverse)


def transposed(features, weight_one, bias_one, weight_two, bias_two, cotangent, neighbours, valid_mask):
    nodes, full = features.shape
    chip_rows, cols = lax.axis_size("ch"), lax.axis_size("col")
    chips = chip_rows * cols
    core = lax.axis_index("core")
    col = lax.axis_index("col")
    row = (2 * lax.axis_index("ch") + core).reshape(1)
    every = ("ch", "col")

    def swap(value):
        return lax.ppermute(value, "core", [(0, 1), (1, 0)])

    def across(value, mask):
        return lax.ppermute(value, "ch", [(i, i ^ mask) for i in range(chip_rows)])

    def exchange(value):
        return lax.all_to_all(value, every, 0, 0, tiled=True)

    at = jnp.concatenate([row, col.reshape(1)])

    lists = neighbours.reshape(-1, MXU)
    lists = jnp.stack([lists] + [across(lists, mask) for mask in range(1, chip_rows)])
    own = exchange(jnp.transpose(features.reshape(nodes, chips, LANES), (1, 0, 2)))
    turned = count_tile(at, lists, nodes, cols, True)
    tile_own = count_tile(at, lists, nodes, cols, False)
    tile_other = count_tile(at, swap(lists), nodes, cols, False)

    own_lists = lax.dynamic_slice_in_dim(neighbours, col * nodes, nodes, 0)
    inverse = 1.0 / (jnp.sum(own_lists >= 0, axis=1).astype(F32) + 1.0)
    inverse = inverse.reshape(1, nodes)
    valid = valid_mask.astype(F32).reshape(nodes, 1)

    def to_plane(parts):
        return [parts[0]] + [across(parts[mask], mask) for mask in range(1, chip_rows)]

    def both_cores(parts):
        return [part for one in parts for part in (one, swap(one))]

    def along(value, mask):
        return lax.ppermute(value, "col", [(i, i ^ mask) for i in range(cols)])

    def exchange_beside(value, *others):
        return lax.optimization_barrier((exchange(value), *others))

    own, turned = lax.optimization_barrier((own, turned))
    agg_one = exchange(apply_adjacency([turned], own, swap(own), True))
    agg_one, tile_own = lax.optimization_barrier((agg_one, tile_own))
    hidden, slope_one, stats_one, *pieces_one = first_layer(
        at, agg_one, weight_one, bias_one.reshape(1, -1), valid, features, chip_rows
    )
    own, tile_other = exchange_beside(hidden, tile_other)
    agg_two = apply_adjacency([turned], own, swap(own), True)
    agg_two, *pieces_one = exchange_beside(agg_two, *to_plane(pieces_one))
    act, grad_pre_two, sums_two, grad_agg_two, *pieces_two = second_layer(
        at, agg_two, weight_two, bias_two.reshape(1, -1), valid, cotangent, inverse, stats_one, chip_rows
    )
    cut = nodes // 2

    def backward_one(grads, grad_pre, *others):
        own, by_x, by_y, core_other, *others = exchange_beside(
            grads, across(grad_pre, 1), across(grad_pre, 2), swap(grad_pre), *others
        )
        diagonal = across(by_x, 2)
        sums = apply_adjacency([tile_own, tile_other], own, swap(own), False)
        sums, by_x, by_y = lax.optimization_barrier((sums, by_x, by_y))
        return sums, [grad_pre, core_other, *both_cores([by_x, by_y, diagonal])], others

    def backward_two(grads, grad_pre, *others):
        own, by_x, by_y, core_other, *others = exchange_beside(
            grads, across(grad_pre, 1), across(grad_pre, 2), swap(grad_pre), *others
        )
        diagonal = [across(by_x[:cut], 2), across(by_y[cut:], 1)]
        sums = apply_adjacency([tile_own, tile_other], own, swap(own), False)
        sums, by_x, by_y, *diagonal = lax.optimization_barrier((sums, by_x, by_y, *diagonal))
        return sums, [grad_pre, core_other, *both_cores([by_x, by_y]), *both_halves(diagonal)], others

    def both_halves(diagonal):
        return diagonal + [swap(part) for part in diagonal]

    sums, plane_two, _ = backward_two(sums_two, grad_pre_two)
    sums, *pieces_two = lax.optimization_barrier((sums, *pieces_two))
    upstream, *pieces_two = exchange_beside(sums, *to_plane(pieces_two))
    grad_pre_one, sums_one, grad_agg_one = first_layer_back(slope_one, weight_one, inverse, upstream, grad_agg_two)
    kept_two, sent_two = weight_product(at, both_cores(pieces_two), plane_two, ((0, 2), (1, 3)))
    sums, plane_one, (kept_two, sent_two) = backward_one(sums_one, grad_pre_one, kept_two, sent_two)
    grad_start = input_gradient(exchange(sums), grad_agg_one, inverse)
    pair_two = along(sent_two, 1)
    last_two, plane_one[0] = lax.optimization_barrier((pair_sum(kept_two, pair_two), plane_one[0]))
    last_two = along(last_two, 2)
    parts_one = weight_product(at, both_cores(pieces_one), plane_one, tuple((mask,) for mask in range(cols)))
    parts_one = [part if mask == 0 else along(part, mask) for mask, part in enumerate(parts_one)]
    last_two, grad_start = lax.optimization_barrier((last_two, grad_start))
    weight_grad_two, bias_grad_two, rms_stats = sum_pieces([kept_two, pair_two, last_two])
    *parts_one, weight_grad_two = lax.optimization_barrier((*parts_one, weight_grad_two))
    weight_grad_one, bias_grad_one, _ = sum_pieces(parts_one)
    bias_grad_one, bias_grad_two = bias_grad_one.reshape(-1), bias_grad_two.reshape(-1)
    return (act, grad_start, weight_grad_one, bias_grad_one, weight_grad_two, bias_grad_two, rms_stats)


def solution(mesh):
    rows, cols = mesh.devices.shape
    axes = ("ch", "core", "col")
    wide = Mesh(mesh.devices.reshape(rows // 2, 2, cols), axes)

    def program(features, *rest):
        nodes, full = features.shape
        slots = rest[5].shape[1]
        fits = (
            (rows, cols) == (8, 4)
            and nodes == rows * cols * LANES
            and full == rows * cols * 64
            and slots * nodes == MXU * MXU
            and slots == 16
        )
        split, over = (axes, wide) if fits else (("row", "col"), mesh)
        lists = ("ch", "core") if fits else "row"
        spread = P(split, None)
        return jax.shard_map(
            transposed if fits else general,
            mesh=over,
            in_specs=(spread, P(), P(), P(), P(), spread, P(lists, None), P(split)),
            out_specs=(spread, spread, spread, P(split), spread, P(split), P()),
            check_vma=False,
        )(features, *rest)

    return program
```

```python
import functools

import jax
import jax.numpy as jnp
from jax import lax
from jax.experimental import pallas as pl
from jax.experimental.pallas import tpu as pltpu
from jax.sharding import Mesh
from jax.sharding import PartitionSpec as P

BF16, F32 = jnp.bfloat16, jnp.float32
LANES = 128
MXU = 256
MIB = 1 << 20
NT = (((1,), (1,)), ((), ()))
GELU_C, GELU_A = 0.7978845608, 0.044715


def gelu_value(value):
    return jax.nn.gelu(value, approximate=True)


def source_parts(lists, per_dev, col_devs):
    live = lists >= 0
    safe = jnp.maximum(lists, 0)
    block = safe // per_dev
    return (live, block // col_devs, block % col_devs, safe % per_dev)


def block_tile(lists, usable, local_index, span):
    columns = jnp.arange(span, dtype=jnp.int32)[None, :]
    marked = jnp.where(usable, local_index, -1)
    total = jnp.zeros((lists.shape[0], span), jnp.float32)
    for slot in range(lists.shape[1]):
        total = total + (marked[:, slot : slot + 1] == columns).astype(jnp.float32)
    return total.astype(jnp.bfloat16)


def reduce_weights(grad_weight, grad_bias):
    return (
        lax.psum_scatter(grad_weight, ("row", "col"), scatter_dimension=0, tiled=True),
        lax.psum_scatter(grad_bias, ("row", "col"), scatter_dimension=0, tiled=True),
    )


def general(features, weight_one, bias_one, weight_two, bias_two, cotangent, neighbours, valid_mask):
    per_dev, width = features.shape
    row_devs = lax.axis_size("row")
    col_devs = lax.axis_size("col")
    col_pos = lax.axis_index("col")
    own_lists = lax.dynamic_slice_in_dim(neighbours, col_pos * per_dev, per_dev, 0)
    inverse = 1.0 / (jnp.sum(own_lists >= 0, axis=1).astype(jnp.float32) + 1.0)
    scaling = inverse[:, None]
    validity = valid_mask.astype(jnp.float32)[:, None]
    live, src_row, src_col, offset = source_parts(neighbours, per_dev, col_devs)
    front_tile = block_tile(
        neighbours, live & (src_col == col_pos), src_row * per_dev + offset, row_devs * per_dev
    )

    def forward_layer(inputs, weight, bias):
        gathered = lax.all_gather(inputs, "row", axis=0, tiled=True)
        partial_value = jnp.dot(front_tile, gathered, preferred_element_type=jnp.float32)
        summed = lax.psum_scatter(partial_value, "col", scatter_dimension=0, tiled=True)
        aggregate = ((summed + 2.0 * inputs.astype(jnp.float32)) * scaling).astype(jnp.bfloat16)
        preact = jnp.dot(aggregate, weight, preferred_element_type=jnp.float32) + bias
        return (aggregate, preact, validity * gelu_value(preact))

    agg_one, pre_one, out_one = forward_layer(features, weight_one, bias_one)
    hidden = out_one.astype(jnp.bfloat16)
    agg_two, pre_two, out_two = forward_layer(hidden, weight_two, bias_two)

    def squares(value):
        return jnp.sum(validity * jnp.square(value.astype(jnp.float32)))

    local_squares = jnp.stack(
        [
            squares(features),
            squares(agg_one),
            squares(out_one),
            squares(hidden),
            squares(agg_two),
            squares(out_two),
        ]
    ).reshape(2, 3)
    total_squares, total_valid = lax.psum((local_squares, jnp.sum(validity)), ("row", "col"))
    rms_stats = jnp.sqrt(total_squares / (total_valid * width) + 1e-06)

    def backward_layer(upstream, aggregate, preact, weight):
        grad_act = validity * upstream
        grad_pre = jax.vjp(gelu_value, preact)[1](grad_act)[0].astype(jnp.bfloat16)
        grad_weight = lax.dot_general(
            aggregate, grad_pre, (((0,), (0,)), ((), ())), preferred_element_type=jnp.float32
        )
        grad_bias = jnp.sum(grad_pre.astype(jnp.float32), axis=0)
        grad_low = lax.dot_general(
            grad_pre, weight, (((1,), (1,)), ((), ())), preferred_element_type=jnp.float32
        ).astype(jnp.bfloat16)
        grad_agg = lax.optimization_barrier(grad_low).astype(jnp.float32)
        grad_sum = (grad_agg * scaling).astype(jnp.bfloat16)
        grad_all = lax.all_gather(grad_sum, "col", axis=0, tiled=True)
        from_lists = lax.psum_scatter(
            lax.dot_general(
                front_tile, grad_all, (((0,), (0,)), ((), ())), preferred_element_type=jnp.float32
            ),
            "row",
            scatter_dimension=0,
            tiled=True,
        )
        return (from_lists + 2.0 * grad_agg * scaling, grad_weight, grad_bias)

    grad_hidden, weight_grad_two, bias_grad_two = backward_layer(
        cotangent.astype(jnp.float32), agg_two, pre_two, weight_two
    )
    weight_grad_two, bias_grad_two = reduce_weights(weight_grad_two, bias_grad_two)
    grad_start, weight_grad_one, bias_grad_one = backward_layer(
        grad_hidden, agg_one, pre_one, weight_one
    )
    weight_grad_one, bias_grad_one = reduce_weights(weight_grad_one, bias_grad_one)
    return (
        out_two.astype(jnp.bfloat16),
        grad_start.astype(jnp.bfloat16),
        weight_grad_one,
        bias_grad_one,
        weight_grad_two,
        bias_grad_two,
        rms_stats,
    )


IN_VMEM = pl.BlockSpec(memory_space=pltpu.VMEM)
IN_SMEM = pl.BlockSpec(memory_space=pltpu.SMEM)
IN_ANY = pl.BlockSpec(memory_space=pl.ANY)
COUNT = jnp.float8_e4m3fn
PARAMS = pltpu.CompilerParams(vmem_limit_bytes=51 * MIB)
WIDE = pltpu.CompilerParams(vmem_limit_bytes=62 * MIB)


def cost(flops, read, transcendentals=0):
    return pl.CostEstimate(flops=flops, bytes_accessed=read, transcendentals=transcendentals)


def lanes(at, size=LANES):
    return slice(at * size, (at + 1) * size)


def fetch(source, target, semaphore):
    copy = pltpu.make_async_copy(source, target, semaphore)
    copy.start()
    return copy


def stream(source, blocks, target, semaphores):
    copies = [fetch(source.at[block], target.at[block], semaphores.at[i]) for i, block in enumerate(blocks)]

    def arrivals():
        for block, copy in zip(blocks, copies, strict=True):
            copy.wait()
            yield target[block]

    return arrivals()


def buffer(shape, blocks, dtype=BF16):
    return [pltpu.VMEM(shape, dtype), pltpu.SemaphoreType.DMA((blocks,))]


def like(value):
    return [pltpu.VMEM(value.shape, value.dtype), pltpu.SemaphoreType.DMA]


class Results:
    def __init__(self, semaphores):
        self.semaphores, self.copies = semaphores, []

    def send(self, source, target):
        self.copies.append(fetch(source, target, self.semaphores.at[len(self.copies)]))

    def wait(self):
        for copy in self.copies:
            copy.wait()


def column_blocks(size, step):
    return [(slice(None), slice(at, at + step)) for at in range(0, size, step)]


def row_blocks(size, step):
    return [(slice(at, at + step), slice(None)) for at in range(0, size, step)]


def tile_kernel(turn, nodes, cols, place_ref, lists_ref, tile_ref):
    masks, lines, width = lists_ref.shape
    groups = 8
    rows = LANES // groups
    chip_row, core = place_ref[0] // 2, place_ref[0] % 2
    step = pl.program_id(0)
    per_chip = lines // groups
    mask = chip_row ^ (step // per_chip)
    lists = lists_ref[mask, pl.ds(pl.multiple_of(step % per_chip * groups, groups), groups), :]
    node_bits, col_bits = nodes.bit_length() - 1, cols.bit_length() - 1
    owner_row = lists >> (node_bits + col_bits)
    within = lists & (nodes * cols - 1)
    place = ((owner_row >> 1) << (node_bits + col_bits)) + within
    live = lists >= 0
    if turn:
        half = masks * cols * nodes
        place = jnp.where((owner_row & 1) == core, place, place + half)
    else:
        live &= (owner_row & 1) == core
    line = lax.broadcasted_iota(jnp.int32, lists.shape, 1) // rows
    highs = jnp.where(live, (place // MXU) * rows + line, -1)
    lows = place % MXU
    blocks = (tile_ref.shape[0] if turn else tile_ref.shape[1]) // MXU
    high_place = lax.broadcasted_iota(jnp.int32, (blocks * rows, width), 0)
    low_place = lax.broadcasted_iota(jnp.int32, (MXU, width), 0)
    pieces = []
    for group in range(groups):
        high = (high_place == highs[group : group + 1, :]).astype(F32).astype(BF16)
        low = (low_place == lows[group : group + 1, :]).astype(F32).astype(BF16)
        counts = lax.dot_general(high, low, NT, preferred_element_type=F32)
        pieces.append(counts.astype(BF16))
    for block in range(blocks):
        column = jnp.concatenate([piece[block * rows : (block + 1) * rows] for piece in pieces], axis=0)
        if turn:
            for side in range(2):
                turned = column[:, lanes(side)].T
                tile_ref[lanes(2 * block + side), :] = turned.astype(COUNT)
        else:
            tile_ref[:, lanes(block, MXU)] = column.astype(COUNT)


def count_tile(at, lists, nodes, cols, turn):
    masks, lines, width = lists.shape
    rows = masks * lines * 16
    half = masks * cols * nodes
    shape = (2 * half, rows) if turn else (rows, half)
    block = (2 * half, LANES) if turn else (LANES, half)
    return pl.pallas_call(
        functools.partial(tile_kernel, turn, nodes, cols),
        grid=(rows // LANES,),
        in_specs=[IN_SMEM, pl.BlockSpec(lists.shape, lambda i: (0, 0, 0))],
        out_specs=pl.BlockSpec(block, (lambda i: (0, i)) if turn else (lambda i: (i, 0))),
        out_shape=jax.ShapeDtypeStruct(shape, COUNT),
        compiler_params=PARAMS,
        cost_estimate=cost(4 * rows * shape[0 if turn else 1] * 2 * MXU, rows * half),
    )(at, lists)


def adjacency_kernel(forward, tiles, own_ref, other_ref, *refs):
    tile_refs, refs = refs[:tiles], refs[-10 - tiles :]
    out_ref, left_ref, total_ref, own, own_sem, other, other_sem = refs[:7]
    buffers, (semaphores, out, out_sems) = refs[7 : 7 + tiles], refs[7 + tiles :]
    chips, width = own_ref.shape[0], LANES
    half = chips * width
    copies = [fetch(own_ref, own, own_sem), fetch(other_ref, other, other_sem)]
    chunks, arrivals = [], []
    for ref, target in zip(tile_refs, buffers, strict=True):
        for at in range(0, ref.shape[0], half):
            here = slice(at, at + half)
            arrivals.append(fetch(ref.at[here], target.at[here], semaphores.at[len(chunks)]))
            chunks.append(target.at[here])
    for copy in copies:
        copy.wait()
    for at in range(chips):
        left_ref[:width, lanes(at)] = own[at].T if forward else own[at]
        left_ref[:width, lanes(chips + at)] = other[at].T if forward else other[at]
    if forward:
        left_ref[width:, :] = jnp.ones((left_ref.shape[0] - width, left_ref.shape[1]), BF16)
    for block, (copy, counts) in enumerate(zip(arrivals, chunks, strict=True)):
        copy.wait()
        part = jnp.dot(left_ref[:, lanes(block, half)], counts[...].astype(BF16), preferred_element_type=F32)
        if block == 0:
            total_ref[...] = part
        else:
            total_ref[...] += part
    results = Results(out_sems)
    group = chips // out_sems.shape[0]
    for at in range(chips):
        here = lanes(at)
        if forward:
            inverse = 1.0 / (total_ref[width : width + 1, here] + 1.0)
            value = (total_ref[:width, here] + 2.0 * left_ref[:width, here].astype(F32)) * inverse
            out[at] = value.astype(BF16).T
        else:
            out[at] = total_ref[:, here].astype(BF16)
        if (at + 1) % group == 0:
            done = slice(at + 1 - group, at + 1)
            results.send(out.at[done], out_ref.at[done])
    results.wait()


def apply_adjacency(tiles, own, other, forward, *after):
    sources, half = sum(tile.shape[0] for tile in tiles), tiles[0].shape[1]
    rows = LANES + (16 if forward else 0)
    scratch = [pltpu.VMEM((rows, sources), BF16), pltpu.VMEM((rows, half), F32)] + like(own) + like(other)
    scratch += [pltpu.VMEM(tile.shape, COUNT) for tile in tiles] + [pltpu.SemaphoreType.DMA((sources // half,))]
    return pl.pallas_call(
        functools.partial(adjacency_kernel, forward, len(tiles)),
        in_specs=[IN_ANY] * (2 + len(tiles) + len(after)),
        out_specs=IN_ANY,
        out_shape=jax.ShapeDtypeStruct(own.shape, BF16),
        scratch_shapes=scratch + buffer(own.shape, 4),
        compiler_params=PARAMS,
        cost_estimate=cost(2 * half * sources * LANES, half * sources),
    )(own, other, *tiles, *after)


def gelu_parts(pre, valid):
    square = pre * pre
    bend = jnp.tanh(GELU_C * (pre + GELU_A * (square * pre)))
    inner = GELU_C * (1.0 + 3.0 * GELU_A * square)
    slope = 0.5 * (1.0 + bend) + 0.5 * pre * (1.0 - bend * bend) * inner
    return valid * (0.5 * pre * (1.0 + bend)), valid * slope


def lane_squares(value, valid):
    value = value.astype(F32)
    value = jnp.sum(valid * (value * value), axis=0, keepdims=True)
    return sum(value[:, lanes(i)] for i in range(value.shape[1] // LANES))


def send_pieces(at_ref, agg_blocks, pieces, piece_refs, results):
    chip_row = at_ref[0] // 2
    blocks = agg_blocks.shape[0] // len(piece_refs)
    for mask, ref in enumerate(piece_refs):
        for part in range(blocks):
            pieces[mask, :, lanes(part)] = agg_blocks[(chip_row ^ mask) * blocks + part]
        results.send(pieces.at[mask], ref)


def first_kernel(at_ref, agg_ref, weight_ref, bias_ref, valid_ref, input_ref, *refs):
    out_ref, slope_ref, stat_ref = refs[-17:-14]
    piece_refs = refs[-14:-10]
    agg_blocks, agg_sem, inputs, input_sem, weight_buffer, semaphores = refs[-10:-4]
    out, slopes, pieces, out_sems = refs[-4:]
    chips, nodes, width = agg_ref.shape
    full = weight_ref.shape[1]
    step = full // semaphores.shape[0]
    copies = [fetch(agg_ref, agg_blocks, agg_sem)]
    weights = stream(weight_ref, column_blocks(full, step), weight_buffer, semaphores)
    copies.append(fetch(input_ref, inputs, input_sem))
    results = Results(out_sems)
    valid = valid_ref[...]
    copies[0].wait()
    agg = jnp.concatenate([agg_blocks[i] for i in range(chips)], axis=1)
    send_pieces(at_ref, agg_blocks, pieces, piece_refs, results)
    none = jnp.zeros((1, LANES), F32)
    of_agg, of_input, of_out, of_low = lane_squares(agg, valid), none, none, none
    for block, weight in enumerate(weights):
        here = lanes(block, step)
        pre = jnp.dot(agg, weight, preferred_element_type=F32) + bias_ref[:, here]
        value, slopes[:, here] = gelu_parts(pre, valid)
        low = value.astype(BF16)
        of_out += lane_squares(value, valid)
        of_low += lane_squares(low, valid)
        if block == 0:
            copies[1].wait()
        of_input += lane_squares(inputs[:, here], valid)
        blocks = lanes(block, step // LANES)
        for part in range(step // LANES):
            out[blocks.start + part] = low[:, lanes(part)]
        results.send(out.at[blocks], out_ref.at[blocks])
        results.send(slopes.at[:, here], slope_ref.at[:, here])
    count = jnp.sum(jnp.broadcast_to(valid, (nodes, LANES)), axis=0, keepdims=True) * (1.0 / LANES)
    stat_ref[...] = jnp.concatenate([of_input, of_agg, of_out, of_low, count, none, none, none], axis=0)
    results.wait()


def piece_shapes(agg, chip_rows):
    chips, nodes, width = agg.shape
    return [jax.ShapeDtypeStruct((nodes, chips * width // chip_rows), BF16)] * chip_rows


def first_layer(at, agg, weight, bias, valid, inputs, chip_rows, *after):
    chips, nodes, width = agg.shape
    full = weight.shape[1]
    pieces = piece_shapes(agg, chip_rows)
    steps = 2
    return pl.pallas_call(
        first_kernel,
        in_specs=[IN_SMEM, IN_ANY, IN_ANY, IN_VMEM, IN_VMEM, IN_ANY] + [IN_ANY] * len(after),
        out_specs=[IN_ANY, IN_ANY, IN_VMEM] + [IN_ANY] * chip_rows,
        out_shape=[
            jax.ShapeDtypeStruct(agg.shape, BF16),
            jax.ShapeDtypeStruct((nodes, full), F32),
            jax.ShapeDtypeStruct((8, LANES), F32),
        ]
        + pieces,
        scratch_shapes=like(agg)
        + like(inputs)
        + buffer(weight.shape, steps)
        + [
            pltpu.VMEM(agg.shape, BF16),
            pltpu.VMEM((nodes, full), F32),
            pltpu.VMEM((chip_rows,) + pieces[0].shape, BF16),
            pltpu.SemaphoreType.DMA((chip_rows + 2 * steps,)),
        ],
        compiler_params=PARAMS,
        cost_estimate=cost(2 * nodes * full * full, 2 * full * full, nodes * full),
    )(at, agg, weight, bias, valid, inputs, *after)


def gradient_blocks(weight, blocks, turned, inverse, outs, refs, results):
    low = jnp.dot(weight, turned[...], preferred_element_type=F32).astype(BF16)
    sums = (low.astype(F32) * inverse).astype(BF16)
    for value, out, ref in zip((sums, low), outs, refs, strict=True):
        for part in range(weight.shape[0] // LANES):
            out[blocks.start + part] = value[lanes(part)]
        results.send(out.at[blocks], ref.at[blocks])


def second_kernel(
    at_ref, agg_ref, weight_ref, bias_ref, valid_ref, cotangent_ref, inverse_ref, stat_ref, *refs
):
    act_ref, pre_ref, sums_ref, grad_agg_ref = refs[-21:-17]
    piece_refs = refs[-17:-13]
    agg_blocks, agg_sem, cotangent, cotangent_sem, weight_buffer, semaphores = refs[-13:-7]
    act, pres, turned, sums, grad_agg, pieces, out_sems = refs[-7:]
    chips, nodes, width = agg_ref.shape
    full = weight_ref.shape[1]
    step = full // semaphores.shape[0]
    copies = [fetch(agg_ref, agg_blocks, agg_sem)]
    weights = stream(weight_ref, column_blocks(full, step), weight_buffer, semaphores)
    copies.append(fetch(cotangent_ref, cotangent, cotangent_sem))
    results = Results(out_sems)
    valid, inverse = valid_ref[...], inverse_ref[...]
    copies[0].wait()
    agg = jnp.concatenate([agg_blocks[i] for i in range(chips)], axis=1)
    send_pieces(at_ref, agg_blocks, pieces, piece_refs, results)
    of_agg, of_out = lane_squares(agg, valid), jnp.zeros((1, LANES), F32)
    for block, weight in enumerate(weights):
        here = lanes(block, step)
        pre = jnp.dot(agg, weight, preferred_element_type=F32) + bias_ref[:, here]
        value, slope = gelu_parts(pre, valid)
        of_out += lane_squares(value, valid)
        act[:, here] = value.astype(BF16)
        results.send(act.at[:, here], act_ref.at[:, here])
        if block == 0:
            copies[1].wait()
        grad_pre = (cotangent[:, here].astype(F32) * slope).astype(BF16)
        pres[:, here] = grad_pre
        for part in range(step // LANES):
            turned[block * step + part * LANES : block * step + (part + 1) * LANES, :] = grad_pre[:, lanes(part)].T
    stat = stat_ref[...]
    rows = [stat[:4], of_agg, of_out, stat[4:5], jnp.zeros((1, LANES), F32)]
    total = jnp.sum(jnp.concatenate(rows, axis=0), axis=1, keepdims=True)
    high = total.astype(BF16).astype(F32)
    both = jnp.concatenate([high, total - high], axis=0)
    pres[:16, full:] = jnp.broadcast_to(both, (16, LANES)).astype(BF16)
    pres[16:, full:] = jnp.zeros((nodes - 16, LANES), BF16)
    results.send(pres, pre_ref)
    step = full // 4
    for block in range(4):
        gradient_blocks(
            weight_buffer[lanes(block, step), :], lanes(block, step // LANES), turned, inverse,
            (sums, grad_agg), (sums_ref, grad_agg_ref), results,
        )
    results.wait()


def second_layer(at, agg, weight, bias, valid, cotangent, inverse, stats, chip_rows, *after):
    chips, nodes, width = agg.shape
    full = weight.shape[1]
    blocks = jax.ShapeDtypeStruct((chips, width, nodes), BF16)
    pieces = piece_shapes(agg, chip_rows)
    steps = 2
    return pl.pallas_call(
        second_kernel,
        in_specs=[IN_SMEM, IN_ANY, IN_ANY, IN_VMEM, IN_VMEM, IN_ANY, IN_VMEM, IN_VMEM] + [IN_ANY] * len(after),
        out_specs=[IN_ANY] * (4 + chip_rows),
        out_shape=[
            jax.ShapeDtypeStruct((nodes, full), BF16),
            jax.ShapeDtypeStruct((nodes, full + LANES), BF16),
            blocks,
            blocks,
        ]
        + pieces,
        scratch_shapes=like(agg)
        + like(cotangent)
        + buffer(weight.shape, steps)
        + [
            pltpu.VMEM((nodes, full), BF16),
            pltpu.VMEM((nodes, full + LANES), BF16),
            pltpu.VMEM((full, nodes), BF16),
            pltpu.VMEM(blocks.shape, BF16),
            pltpu.VMEM(blocks.shape, BF16),
            pltpu.VMEM((chip_rows,) + pieces[0].shape, BF16),
            pltpu.SemaphoreType.DMA((chip_rows + steps + 1 + 8,)),
        ],
        compiler_params=WIDE,
        cost_estimate=cost(4 * nodes * full * full, 2 * full * full, nodes * full),
    )(at, agg, weight, bias, valid, cotangent, inverse, stats, *after)


def back_kernel(slope_ref, weight_ref, inverse_ref, up_ref, extra_ref, *refs):
    pre_ref, sums_ref, agg_ref, slope, slope_sem, up, up_sem, extra, extra_sem = refs[-16:-7]
    weight_buffer, semaphores, pres, turned, sums, grad_agg, out_sems = refs[-7:]
    nodes, full = slope_ref.shape
    step = full // semaphores.shape[0]
    copies = [fetch(up_ref, up, up_sem), fetch(extra_ref, extra, extra_sem), fetch(slope_ref, slope, slope_sem)]
    weights = stream(weight_ref, row_blocks(full, step), weight_buffer, semaphores)
    results = Results(out_sems)
    inverse = inverse_ref[...]
    for copy in copies:
        copy.wait()
    for at in range(up_ref.shape[0]):
        value = up[at].astype(F32) + 2.0 * extra[at].astype(F32) * inverse
        grad_pre = (value.T * slope[:, lanes(at)]).astype(BF16)
        pres[:, lanes(at)] = grad_pre
        turned[lanes(at), :] = grad_pre.T
    pres[:, full:] = jnp.zeros((nodes, LANES), BF16)
    results.send(pres, pre_ref)
    for block, weight in enumerate(weights):
        gradient_blocks(
            weight, lanes(block, step // LANES), turned, inverse, (sums, grad_agg), (sums_ref, agg_ref), results
        )
    results.wait()


def first_layer_back(slope, weight, inverse, upstream, extra, *after):
    nodes, full = slope.shape
    blocks = jax.ShapeDtypeStruct(upstream.shape, BF16)
    steps = 1
    return pl.pallas_call(
        back_kernel,
        in_specs=[IN_ANY, IN_ANY, IN_VMEM, IN_ANY, IN_ANY] + [IN_ANY] * len(after),
        out_specs=[IN_ANY] * 3,
        out_shape=[jax.ShapeDtypeStruct((nodes, full + LANES), BF16), blocks, blocks],
        scratch_shapes=like(slope)
        + like(upstream)
        + like(extra)
        + buffer(weight.shape, steps)
        + [
            pltpu.VMEM((nodes, full + LANES), BF16),
            pltpu.VMEM((full, nodes), BF16),
            pltpu.VMEM(blocks.shape, BF16),
            pltpu.VMEM(blocks.shape, BF16),
            pltpu.SemaphoreType.DMA((1 + 2 * steps,)),
        ],
        compiler_params=PARAMS,
        cost_estimate=cost(2 * nodes * full * full, 2 * full * full),
    )(slope, weight, inverse, upstream, extra, *after)


def left_factor(at_ref, lefts, left_parts, left_sem, left_ref):
    nodes = lefts[0].shape[0]
    width = left_parts.shape[2]
    mine = pl.ds(pl.multiple_of(at_ref[0] % 2 * width, width), width)
    copies = [fetch(ref.at[:, mine], left_parts.at[i], left_sem.at[i]) for i, ref in enumerate(lefts)]

    def finish():
        for i, copy in enumerate(copies):
            copy.wait()
            left_ref[:width, lanes(i, nodes)] = left_parts[i].T
        left_ref[width:, :] = jnp.ones((left_ref.shape[0] - width, left_ref.shape[1]), BF16)

    return finish


def products(at_ref, left_ref, right, copies, width, use):
    bias = jnp.zeros((8, width), F32)
    step = right.shape[1] // len(copies)
    for block, group in enumerate(copies):
        for copy in group:
            copy.wait()
        here = lanes(block, step)
        total = jnp.dot(left_ref[...], right[:, here], preferred_element_type=F32)
        use(here, total)
        for part in range(step // width):
            one = block * (step // width) + part
            bias += jnp.where(at_ref[0] == one, total[width : width + 8, lanes(part, width)], 0.0)
    return bias


def small_sums(bias, stats, rows):
    high, stats_high = bias.astype(BF16).astype(F32), stats.astype(BF16).astype(F32)
    line = lax.broadcasted_iota(jnp.int32, (8, LANES), 0)
    first = jnp.where(line == 0, high, jnp.where(line == 1, bias - high, 0.0))
    rest = jnp.zeros((rows - 24, LANES), F32)
    return jnp.concatenate([first, stats_high, stats - stats_high, rest], axis=0).astype(BF16)


def read_small(extra):
    return extra[0:1] + extra[1:2], extra[8:16] + extra[16:24]


def weight_kernel(masks, at_ref, *refs):
    lefts, rights, outs = refs[:8], refs[8 : -7 - len(masks)], refs[-7 - len(masks) : -7]
    left_parts, left_sem, right, right_sems, stat_parts, stat_sems, left_ref = refs[-7:]
    col = at_ref[1]
    full = outs[0].shape[1] - LANES
    piece_rows = outs[0].shape[0] // len(masks[0])
    pieces = sum(len(group) for group in masks)
    nodes, width = left_parts.shape[1:]
    finish = left_factor(at_ref, lefts, left_parts, left_sem, left_ref)
    steps = right_sems.shape[0]
    starts = [sum(ref.shape[0] for ref in rights[:i]) for i in range(len(rights))]
    copies = [
        [
            fetch(
                ref.at[:, lanes(block, full // steps)],
                right.at[slice(start, start + ref.shape[0]), lanes(block, full // steps)],
                right_sems.at[block, i],
            )
            for i, (ref, start) in enumerate(zip(rights, starts, strict=True))
        ]
        for block in range(steps)
    ]
    firsts = [ref for ref, start in zip(rights, starts, strict=True) if start % nodes == 0]
    stat_copies = [
        fetch(ref.at[:16, slice(full, full + LANES)], stat_parts.at[i], stat_sems.at[i])
        for i, ref in enumerate(firsts)
    ]
    finish()

    def use(here, total):
        for group, ref in zip(masks, outs, strict=True):
            for at, mask in enumerate(group):
                value = total[:piece_rows]
                for piece in range(1, pieces):
                    value = jnp.where(col ^ mask == piece, total[lanes(piece, piece_rows)], value)
                ref[lanes(at, piece_rows), here] = value.astype(BF16)

    bias = products(at_ref, left_ref, right, copies, width, use)
    stats = jnp.zeros((8, LANES), F32)
    for i, copy in enumerate(stat_copies):
        copy.wait()
        both = stat_parts[i].astype(F32)
        stats += both[:8] + both[8:]
    for group, ref in zip(masks, outs, strict=True):
        for at, mask in enumerate(group):
            piece = col ^ mask
            one = jnp.where(piece >= 2, bias[:, LANES:], bias[:, :LANES])
            one = jnp.where(piece % 2 == 1, pltpu.roll(one, LANES // 2, 1), one)
            ref[lanes(at, piece_rows), full:] = small_sums(one, stats, piece_rows)


def weight_product(at, lefts, rights, masks):
    nodes, full = lefts[0].shape[0], rights[0].shape[1]
    full -= LANES
    width = lefts[0].shape[1] // 2
    rows = width // sum(len(group) for group in masks)
    return pl.pallas_call(
        functools.partial(weight_kernel, masks),
        in_specs=[IN_SMEM] + [IN_ANY] * (8 + len(rights)),
        out_specs=[IN_VMEM] * len(masks),
        out_shape=[jax.ShapeDtypeStruct((rows * len(group), full + LANES), BF16) for group in masks],
        scratch_shapes=[
            pltpu.VMEM((8, nodes, width), BF16),
            pltpu.SemaphoreType.DMA((8,)),
            pltpu.VMEM((8 * nodes, full), BF16),
            pltpu.SemaphoreType.DMA((2, len(rights))),
            pltpu.VMEM((8, 16, LANES), BF16),
            pltpu.SemaphoreType.DMA((8,)),
            pltpu.VMEM((width + 16, 8 * nodes), BF16),
        ],
        compiler_params=PARAMS,
        cost_estimate=cost(2 * 8 * nodes * full * width, 4 * 8 * nodes * full),
    )(at, *lefts, *rights)


def pair_kernel(one_ref, two_ref, out_ref):
    rows, full = out_ref.shape
    full -= LANES
    step = 512
    for at in range(0, full, step):
        here = slice(at, at + step)
        out_ref[:, here] = (one_ref[rows:, here].astype(F32) + two_ref[rows:, here].astype(F32)).astype(BF16)
    bias, stats = read_small(one_ref[rows:, full:].astype(F32) + two_ref[rows:, full:].astype(F32))
    out_ref[:, full:] = small_sums(bias, stats, rows)


def pair_sum(one, two):
    return pl.pallas_call(
        pair_kernel,
        in_specs=[IN_VMEM] * 2,
        out_specs=IN_VMEM,
        out_shape=jax.ShapeDtypeStruct((one.shape[0] // 2, one.shape[1]), BF16),
        compiler_params=PARAMS,
    )(one, two)


def sum_kernel(*refs):
    parts, (out_ref, bias_ref, rms_ref) = refs[:-3], refs[-3:]
    rows, full = out_ref.shape
    count = bias_ref.shape[1]

    def total(here):
        return sum([part[:rows, here].astype(F32) for part in parts[1:]], parts[0][:rows, here].astype(F32))

    step = 512
    for at in range(0, full, step):
        out_ref[:, at : at + step] = total(slice(at, at + step))
    bias, stats = read_small(total(slice(full, full + LANES)))
    bias_ref[...] = bias[:, :count]
    rms = jnp.sqrt(stats / jnp.maximum(stats[6:7] * full, 1.0) + 1e-06)
    row = lax.broadcasted_iota(jnp.int32, rms_ref.shape, 0)
    place = 3 * row + lax.broadcasted_iota(jnp.int32, rms_ref.shape, 1)
    value = jnp.zeros(rms_ref.shape, F32)
    for at in range(6):
        value = jnp.where(place == at, rms[at : at + 1, :3], value)
    rms_ref[...] = value


def sum_pieces(parts):
    rows, full = parts[-1].shape
    full -= LANES
    return pl.pallas_call(
        sum_kernel,
        in_specs=[IN_VMEM] * len(parts),
        out_specs=[IN_VMEM] * 3,
        out_shape=[
            jax.ShapeDtypeStruct((rows, full), F32),
            jax.ShapeDtypeStruct((1, rows), F32),
            jax.ShapeDtypeStruct((2, 3), F32),
        ],
        compiler_params=PARAMS,
    )(*parts)


def final_kernel(up_ref, agg_ref, inverse_ref, out_ref):
    inverse = inverse_ref[...]
    for at in range(up_ref.shape[0]):
        value = up_ref[at].astype(F32) + 2.0 * agg_ref[at].astype(F32) * inverse
        out_ref[:, lanes(at)] = value.T.astype(BF16)


def input_gradient(upstream, grad_agg, inverse):
    chips, width, nodes = upstream.shape
    return pl.pallas_call(
        final_kernel,
        in_specs=[IN_VMEM] * 3,
        out_specs=IN_VMEM,
        out_shape=jax.ShapeDtypeStruct((nodes, chips * width), BF16),
        compiler_params=PARAMS,
    )(upstream, grad_agg, inverse)


def transposed(features, weight_one, bias_one, weight_two, bias_two, cotangent, neighbours, valid_mask):
    nodes, full = features.shape
    chip_rows, cols = lax.axis_size("ch"), lax.axis_size("col")
    chips = chip_rows * cols
    core = lax.axis_index("core")
    col = lax.axis_index("col")
    row = (2 * lax.axis_index("ch") + core).reshape(1)
    every = ("ch", "col")

    def swap(value):
        return lax.ppermute(value, "core", [(0, 1), (1, 0)])

    def across(value, mask):
        return lax.ppermute(value, "ch", [(i, i ^ mask) for i in range(chip_rows)])

    def exchange(value):
        return lax.all_to_all(value, every, 0, 0, tiled=True)

    at = jnp.concatenate([row, col.reshape(1)])

    lists = neighbours.reshape(-1, MXU)
    lists = jnp.stack([lists] + [across(lists, mask) for mask in range(1, chip_rows)])
    own = exchange(jnp.transpose(features.reshape(nodes, chips, LANES), (1, 0, 2)))
    turned = count_tile(at, lists, nodes, cols, True)
    tile_own = count_tile(at, lists, nodes, cols, False)
    tile_other = count_tile(at, swap(lists), nodes, cols, False)

    own_lists = lax.dynamic_slice_in_dim(neighbours, col * nodes, nodes, 0)
    inverse = 1.0 / (jnp.sum(own_lists >= 0, axis=1).astype(F32) + 1.0)
    inverse = inverse.reshape(1, nodes)
    valid = valid_mask.astype(F32).reshape(nodes, 1)

    def to_plane(parts):
        return [parts[0]] + [across(parts[mask], mask) for mask in range(1, chip_rows)]

    def both_cores(parts):
        return [part for one in parts for part in (one, swap(one))]

    def along(value, mask):
        return lax.ppermute(value, "col", [(i, i ^ mask) for i in range(cols)])

    def exchange_beside(value, *others):
        return lax.optimization_barrier((exchange(value), *others))

    own, turned = lax.optimization_barrier((own, turned))
    agg_one = exchange(apply_adjacency([turned], own, swap(own), True))
    agg_one, tile_own = lax.optimization_barrier((agg_one, tile_own))
    hidden, slope_one, stats_one, *pieces_one = first_layer(
        at, agg_one, weight_one, bias_one.reshape(1, -1), valid, features, chip_rows
    )
    own, tile_other = exchange_beside(hidden, tile_other)
    agg_two = apply_adjacency([turned], own, swap(own), True)
    agg_two, *pieces_one = exchange_beside(agg_two, *to_plane(pieces_one))
    act, grad_pre_two, sums_two, grad_agg_two, *pieces_two = second_layer(
        at, agg_two, weight_two, bias_two.reshape(1, -1), valid, cotangent, inverse, stats_one, chip_rows
    )
    cut = nodes // 2

    def backward_one(grads, grad_pre, *others):
        own, by_x, by_y, core_other, *others = exchange_beside(
            grads, across(grad_pre, 1), across(grad_pre, 2), swap(grad_pre), *others
        )
        diagonal = across(by_x, 2)
        sums = apply_adjacency([tile_own, tile_other], own, swap(own), False)
        sums, by_x, by_y = lax.optimization_barrier((sums, by_x, by_y))
        return sums, [grad_pre, core_other, *both_cores([by_x, by_y, diagonal])], others

    def backward_two(grads, grad_pre, *others):
        own, by_x, by_y, core_other, *others = exchange_beside(
            grads, across(grad_pre, 1), across(grad_pre, 2), swap(grad_pre), *others
        )
        diagonal = [across(by_x[:cut], 2), across(by_y[cut:], 1)]
        sums = apply_adjacency([tile_own, tile_other], own, swap(own), False)
        sums, by_x, by_y, *diagonal = lax.optimization_barrier((sums, by_x, by_y, *diagonal))
        return sums, [grad_pre, core_other, *both_cores([by_x, by_y]), *both_halves(diagonal)], others

    def both_halves(diagonal):
        return diagonal + [swap(part) for part in diagonal]

    sums, plane_two, _ = backward_two(sums_two, grad_pre_two)
    sums, *pieces_two = lax.optimization_barrier((sums, *pieces_two))
    upstream, *pieces_two = exchange_beside(sums, *to_plane(pieces_two))
    grad_pre_one, sums_one, grad_agg_one = first_layer_back(slope_one, weight_one, inverse, upstream, grad_agg_two)
    kept_two, sent_two = weight_product(at, both_cores(pieces_two), plane_two, ((0, 2), (1, 3)))
    sums, plane_one, (kept_two, sent_two) = backward_one(sums_one, grad_pre_one, kept_two, sent_two)
    grad_start = input_gradient(exchange(sums), grad_agg_one, inverse)
    pair_two = along(sent_two, 1)
    last_two, plane_one[0] = lax.optimization_barrier((pair_sum(kept_two, pair_two), plane_one[0]))
    last_two = along(last_two, 2)
    parts_one = weight_product(at, both_cores(pieces_one), plane_one, tuple((mask,) for mask in range(cols)))
    parts_one = [part if mask == 0 else along(part, mask) for mask, part in enumerate(parts_one)]
    last_two, grad_start = lax.optimization_barrier((last_two, grad_start))
    weight_grad_two, bias_grad_two, rms_stats = sum_pieces([kept_two, pair_two, last_two])
    *parts_one, weight_grad_two = lax.optimization_barrier((*parts_one, weight_grad_two))
    weight_grad_one, bias_grad_one, _ = sum_pieces(parts_one)
    bias_grad_one, bias_grad_two = bias_grad_one.reshape(-1), bias_grad_two.reshape(-1)
    return (act, grad_start, weight_grad_one, bias_grad_one, weight_grad_two, bias_grad_two, rms_stats)


def solution(mesh):
    rows, cols = mesh.devices.shape
    axes = ("ch", "core", "col")
    wide = Mesh(mesh.devices.reshape(rows // 2, 2, cols), axes)

    def program(features, *rest):
        nodes, full = features.shape
        slots = rest[5].shape[1]
        fits = (
            (rows, cols) == (8, 4)
            and nodes == rows * cols * LANES
            and full == rows * cols * 64
            and slots * nodes == MXU * MXU
            and slots == 16
        )
        split, over = (axes, wide) if fits else (("row", "col"), mesh)
        lists = ("ch", "core") if fits else "row"
        spread = P(split, None)
        return jax.shard_map(
            transposed if fits else general,
            mesh=over,
            in_specs=(spread, P(), P(), P(), P(), spread, P(lists, None), P(split)),
            out_specs=(spread, spread, spread, P(split), spread, P(split), P()),
            check_vma=False,
        )(features, *rest)

    return program
```
